256 devices in a mesh: seq: 32 (over x, z_lo, core), var: 4 (over y), mp: 2 (over z_hi).
Axes of the slice: x: 4, y: 4, z: 8 (z_hi: 2, z_lo: 4; z = z_hi * 4 + z_lo), core: 2. Of those that a mesh axis runs over, the one named last changes fastest.
Arguments:
- prefix_input: bfloat16 [16384, 8192], P(('seq', 'var', 'mp')), may hold values from -6 to 6
- prefix_cache: bfloat16 [2, 16384, 8192], P(None, ('seq', 'var', 'mp')), may hold values from -24 to 24
- decay_rates: float32 [8192, 16], replicated, may hold values from 0 to 1, as said below
- residues: float32 [8192, 16], replicated, may hold values from -1 to 1
- suffix_hyena: bfloat16 [2, 8, 512, 8192], P(None, 'var', None, ('seq', 'mp')), may hold values from -6 to 6
- suffix_attn: bfloat16 [3, 8, 512, 8192], P(None, 'var', None, ('seq', 'mp')), may hold values from -24 to 24
- suffix_resid: bfloat16 [8, 512, 8192], P('var', None, ('seq', 'mp')), may hold values from -6 to 6
- norm_gain: float32 [8192], P(('seq', 'mp')), may hold values from 0.1 to 1.9
- readout: bfloat16 [8192, 512], P(('seq', 'mp')), may hold values from -1 to 1
- ref_next: int32 [512], P(('seq', 'mp')), may hold values from 0 to 511
- mutation_pos: int32 [8], P('var'), may hold values from 0 to 511
- mutation_base: int32 [8], P('var'), may hold values from 0 to 511
Outputs:
- logprob: float32 [512, 8], P(('seq', 'mp'), 'var')
The draws below stay inside these ranges and needn't reach their ends.
Inputs may be any that keep to these rules, and one draw needn't show every extreme that they name: `decay_rates`: positive.
All inputs are finite; a program needn't handle non-finite values.
Results may differ from the reference program's by a relative error of at most 0.0045.
Values may be sent and summed in bfloat16 or wider, within the bound.
No kernel may reach another device: no remote copies, remote signals or barrier semaphores. Data moves between devices by JAX's collectives and lax.ppermute only.
A program may use at most 128 MiB of HBM per device.

```python
import jax
import jax.numpy as jnp
from jax import lax

D = 8192
HEADS = 64
HD = 128
VOCAB = 512
MODES = 16
S = 512
L = 16384
VARIANTS = 8
A = 8192


def rate_field(key, slow_share):
    key = jax.random.fold_in(key, 55)
    pick_key, slow_key, fast_key = jax.random.split(key, 3)
    slow_rate = 2.3 / L * jnp.exp(jax.random.uniform(slow_key, (D, MODES), minval=-3.0, maxval=0.0))
    fast_rate = jnp.exp(jax.random.uniform(fast_key, (D, MODES), minval=-3.9, maxval=-2.3))
    return jnp.where(jax.random.uniform(pick_key, (D, MODES)) < slow_share, slow_rate, fast_rate)


def draw_decay_rates(key, part):
    slow_share = 0.5
    rates_drawn = rate_field(key, slow_share)
    return rates_drawn.astype(jnp.float32)


def draw_residues(key, part):
    slow_share = 0.5
    rates_drawn = rate_field(key, slow_share)
    key = jax.random.fold_in(key, 6)
    raw_field = jax.random.normal(key, (D, MODES))
    mode_amps = raw_field * MODES ** (-0.5) * jnp.sqrt(1.0 - jnp.exp(-2.0 * rates_drawn))
    return jnp.clip(mode_amps, -1.0, 1.0).astype(jnp.float32)


def draw_prefix_cache(key, part):
    key = jax.random.fold_in(key, 1)
    scales = jnp.array([1.0, 4.0], jnp.float32)[:, None, None]
    raw_field = jnp.clip(jax.random.normal(key, (2, L, A)), -6.0, 6.0)
    field = raw_field * scales
    return field.astype(jnp.bfloat16)


def draw_suffix_attn(key, part):
    key = jax.random.fold_in(key, 2)
    scales = jnp.array([1.5, 1.0, 4.0], jnp.float32)[:, None, None, None]
    raw_field = jnp.clip(jax.random.normal(key, (3, VARIANTS, S, A)), -6.0, 6.0)
    field = raw_field * scales
    return field.astype(jnp.bfloat16)


def draw_suffix_resid(key, part):
    key = jax.random.fold_in(key, 3)
    field = jnp.clip(jax.random.normal(key, (VARIANTS, S, D)), -6.0, 6.0)
    return field.astype(jnp.bfloat16)


def draw_readout(key, part):
    key = jax.random.fold_in(key, 4)
    column_scale = 3.0 * D ** (-0.5)
    field = jnp.clip(jax.random.normal(key, (D, VOCAB)), -6.0, 6.0) * column_scale
    return jnp.clip(field, -1.0, 1.0).astype(jnp.bfloat16)


def plant(entries, stream_key, least, largest):
    place = [jax.random.randint(jax.random.fold_in(stream_key, axis), (), 0, length) for axis, length in enumerate(entries.shape)]
    widest = entries.shape.index(max(entries.shape))
    neighbour = place[:widest] + [(place[widest] + 1) % entries.shape[widest]] + place[widest + 1:]
    return entries.at[tuple(place)].set(least).at[tuple(neighbour)].set(largest)


def levels(key, dims, cuts, low, high):
    level, own = 1.0, jax.random.fold_in(key, 6)
    for dim, shards_of in cuts:
        heights = jnp.exp(jax.random.uniform(jax.random.fold_in(own, dim), (shards_of,), jnp.float32, low / len(cuts), high / len(cuts)))
        level = level * jnp.repeat(heights, dims[dim] // shards_of).reshape([-1 if axis == dim else 1 for axis in range(len(dims))])
    return level


def scatter_about(key, shape, deviation, most, pieces=(), held_as=jnp.bfloat16):
    values = deviation * jax.random.normal(key, shape, jnp.float32)
    if pieces:
        values = values * levels(key, shape, pieces, -0.22, 0.18)
    return jnp.clip(values, -most, most).astype(held_as)


def setup_inputs(seed: int = 0) -> dict:
    seeds = jax.random.split(jax.random.key(seed), 13)
    prefix_input = scatter_about(seeds[0], (L, D), 1.0, 6.0, ((0, 256),))
    prefix_cache = draw_prefix_cache(jax.random.fold_in(seeds[12], 71), 0)
    decay_rates = draw_decay_rates(jax.random.fold_in(seeds[12], 71), 0)
    residues = draw_residues(jax.random.fold_in(seeds[12], 71), 0)
    suffix_hyena = scatter_about(seeds[4], (2, VARIANTS, S, D), 1.0, 6.0, ((1, 4), (3, 64)))
    suffix_attn = draw_suffix_attn(jax.random.fold_in(seeds[12], 71), 0)
    suffix_resid = draw_suffix_resid(jax.random.fold_in(seeds[12], 71), 0)
    norm_gain = jnp.clip(1.0 + 0.18 * jax.random.normal(seeds[7], (D,), jnp.float32), 0.1, 1.9)
    readout = draw_readout(jax.random.fold_in(seeds[12], 71), 0)
    ref_next = plant(jax.random.randint(seeds[9], (S,), 0, VOCAB), jax.random.fold_in(seeds[9], 1), 0, VOCAB - 1).astype(jnp.int32)
    mutation_pos = plant(jax.random.randint(seeds[10], (VARIANTS,), 0, S), jax.random.fold_in(seeds[10], 1), 0, S - 1).astype(jnp.int32)
    mutation_base = plant(jax.random.randint(seeds[11], (VARIANTS,), 0, VOCAB), jax.random.fold_in(seeds[11], 1), 0, VOCAB - 1).astype(jnp.int32)
    return dict(prefix_input=prefix_input, prefix_cache=prefix_cache, decay_rates=decay_rates, residues=residues, suffix_hyena=suffix_hyena, suffix_attn=suffix_attn, suffix_resid=suffix_resid, norm_gain=norm_gain, readout=readout, ref_next=ref_next, mutation_pos=mutation_pos, mutation_base=mutation_base)


def channel_block():
    if D % 128 == 0:
        return 128
    return D

def prefix_states(prefix_input, decay_rates):
    chan_block = channel_block()
    lag_values = (L - 1 - jnp.arange(L, dtype=jnp.int32)).astype(jnp.float32)

    def one_block(block_id):
        first_row = (block_id * chan_block).astype(jnp.int32)
        log_decay = -lax.dynamic_slice_in_dim(decay_rates, first_row, chan_block, 0)
        inputs = lax.dynamic_slice_in_dim(prefix_input, first_row, chan_block, 1).astype(jnp.float32)
        weights = jnp.exp(log_decay[None, :, :] * lag_values[:, None, None])
        return jnp.einsum('sc,scm->cm', inputs, weights, precision=lax.Precision.HIGHEST)
    blocks = lax.map(one_block, jnp.arange(D // chan_block, dtype=jnp.int32))
    return blocks.reshape(D, MODES)

def suffix_conv(hyena_input, decay_rates, residues, states):
    chan_block = channel_block()
    tap_index = jnp.arange(S, dtype=jnp.int32)
    tap_lag = tap_index[:, None] - tap_index[None, :]
    causal = tap_lag >= 0
    clipped = jnp.maximum(tap_lag, 0)
    tap_float = tap_index.astype(jnp.float32)

    def one_block(block_id):
        first_row = (block_id * chan_block).astype(jnp.int32)
        log_decay = -lax.dynamic_slice_in_dim(decay_rates, first_row, chan_block, 0)
        mode_amps = lax.dynamic_slice_in_dim(residues, first_row, chan_block, 0)
        start_state = lax.dynamic_slice_in_dim(states, first_row, chan_block, 0)
        filter_taps = lax.optimization_barrier(jnp.sum(mode_amps[:, :, None] * jnp.exp(log_decay[:, :, None] * tap_float[None, None, :]), axis=1))
        toeplitz = jnp.where(causal[None], filter_taps[:, clipped], 0.0)
        inputs = lax.dynamic_slice_in_dim(hyena_input, first_row, chan_block, 2).astype(jnp.float32)
        local_part = jnp.einsum('cts,vsc->vtc', toeplitz, inputs, precision=lax.Precision.HIGHEST)
        tail_weights = mode_amps[:, :, None] * jnp.exp(log_decay[:, :, None] * (tap_float + 1.0)[None, None, :])
        tail_part = jnp.einsum('cmt,cm->tc', tail_weights, start_state, precision=lax.Precision.HIGHEST)
        return local_part + tail_part[None]
    blocks = lax.map(one_block, jnp.arange(D // chan_block, dtype=jnp.int32))
    return jnp.moveaxis(blocks, 0, 2).reshape(VARIANTS, S, D)

def attention(suffix_attn, prefix_cache):
    score_scale = HD ** (-0.5)
    queries = suffix_attn[0].reshape(VARIANTS, S, HEADS, HD)
    own_keys = suffix_attn[1].reshape(VARIANTS, S, HEADS, HD)
    own_values = suffix_attn[2].reshape(VARIANTS, S, HEADS, HD)
    prefix_keys = prefix_cache[0].reshape(L, HEADS, HD)
    prefix_values = prefix_cache[1].reshape(L, HEADS, HD)
    positions = jnp.arange(S, dtype=jnp.int32)
    causal = positions[:, None] >= positions[None, :]

    def one_head(head_id):
        query = lax.dynamic_index_in_dim(queries, head_id, 2, keepdims=False).astype(jnp.float32)
        own_key = lax.dynamic_index_in_dim(own_keys, head_id, 2, keepdims=False).astype(jnp.float32)
        own_val = lax.dynamic_index_in_dim(own_values, head_id, 2, keepdims=False).astype(jnp.float32)
        pre_key = lax.dynamic_index_in_dim(prefix_keys, head_id, 1, keepdims=False).astype(jnp.float32)
        pre_val = lax.dynamic_index_in_dim(prefix_values, head_id, 1, keepdims=False).astype(jnp.float32)
        pre_scores = jnp.einsum('vtd,nd->vtn', query, pre_key, precision=lax.Precision.HIGHEST) * score_scale
        own_scores = jnp.einsum('vtd,vsd->vts', query, own_key, precision=lax.Precision.HIGHEST) * score_scale
        own_scores = jnp.where(causal[None], own_scores, -jnp.inf)
        top_score = jnp.maximum(lax.optimization_barrier(jnp.max(pre_scores, axis=-1)), lax.optimization_barrier(jnp.max(own_scores, axis=-1)))
        pre_exp = jnp.exp(pre_scores - top_score[..., None])
        own_exp = jnp.exp(own_scores - top_score[..., None])
        denominator = lax.optimization_barrier(jnp.sum(pre_exp, axis=-1)) + lax.optimization_barrier(jnp.sum(own_exp, axis=-1))
        pre_weights = lax.optimization_barrier(pre_exp.astype(jnp.bfloat16)).astype(jnp.float32)
        own_weights = lax.optimization_barrier(own_exp.astype(jnp.bfloat16)).astype(jnp.float32)
        numer = jnp.einsum('vtn,nd->vtd', pre_weights, pre_val, precision=lax.Precision.HIGHEST)
        numer = numer + jnp.einsum('vts,vsd->vtd', own_weights, own_val, precision=lax.Precision.HIGHEST)
        return numer / denominator[..., None]
    per_head = lax.map(one_head, jnp.arange(HEADS, dtype=jnp.int32))
    return jnp.moveaxis(per_head, 0, 2).reshape(VARIANTS, S, HEADS * HD)

def reference(prefix_input, prefix_cache, decay_rates, residues, suffix_hyena, suffix_attn, suffix_resid, norm_gain, readout, ref_next, mutation_pos, mutation_base):
    states = prefix_states(prefix_input, decay_rates)
    conv_out = suffix_conv(suffix_hyena[1], decay_rates, residues, states)
    hyena_out = suffix_hyena[0].astype(jnp.float32) * conv_out
    attn_out = attention(suffix_attn, prefix_cache)
    hidden = suffix_resid.astype(jnp.float32) + hyena_out + attn_out
    mean_square = lax.optimization_barrier(jnp.mean(hidden * hidden, axis=-1))
    normed = (hidden * lax.rsqrt(mean_square + 1e-05)[..., None] * norm_gain).astype(jnp.bfloat16)
    logits = jnp.dot(normed.reshape(VARIANTS * S, D), readout, preferred_element_type=jnp.float32)
    by_position = jnp.transpose(logits.reshape(VARIANTS, S, VOCAB), (1, 0, 2))
    positions = jnp.arange(S, dtype=jnp.int32)
    target = jnp.where(mutation_pos[None, :] == positions[:, None], mutation_base[None, :], ref_next[:, None])
    picked = jnp.take_along_axis(by_position, target[..., None].astype(jnp.int32), axis=-1)[..., 0]
    return picked - jax.nn.logsumexp(by_position, axis=-1)
```

```python
import functools

import jax
import jax.numpy as jnp
from jax import lax
from jax.experimental import pallas as pl
from jax.experimental.pallas import tpu as pltpu
from jax.sharding import Mesh
from jax.sharding import PartitionSpec as P

D = 8192
HD = 128
MODES = 16
S = 512
LOG2E = 1.4426950408889634
SCALE2 = HD**-0.5 * LOG2E
X, ZL, CORE, Y, ZH = 4, 4, 2, 4, 2
Z = ZL * ZH
GROUPS = X * ZL * CORE * ZH
VPD = 2
ROWS = VPD * S
VOCAB = 512
TILE = 256
SPAN = 512
CHUNK = 128
VMEM_LIMIT = 56 * 1024 * 1024


def params(**kw):
    return pltpu.CompilerParams(vmem_limit_bytes=VMEM_LIMIT, **kw)


def dot_t(a, b):
    return lax.dot_general(a, b, (((1,), (1,)), ((), ())), preferred_element_type=jnp.float32)


def state_kernel(lag_ref, x_ref, rate_ref, out_ref, x32):
    x32[...] = x_ref[...].astype(jnp.float32)
    rate = rate_ref[...]
    decay = jnp.exp(-rate)
    state = jnp.zeros_like(decay)
    for row in range(x_ref.shape[0]):
        state = state * decay + x32[row : row + 1, :]
    state = state * jnp.exp(-rate * lag_ref[0].astype(jnp.float32))
    for zl in range(2):
        for core in range(CORE):
            for zh in range(ZH):
                g = (zl * CORE + core) * ZH + zh
                out_ref[core, 0, zl, zh] = state[:, g * 128 : (g + 1) * 128]


def local_states(lag, prefix_input, rates_t):
    rows = prefix_input.shape[0]
    return pl.pallas_call(
        state_kernel,
        grid=(8,),
        in_specs=[
            pl.BlockSpec(memory_space=pltpu.SMEM),
            pl.BlockSpec((rows, 1024), lambda i: (0, i)),
            pl.BlockSpec((MODES, 1024), lambda i: (0, i)),
        ],
        out_specs=pl.BlockSpec((CORE, 1, 2, ZH, MODES, 128), lambda i: (0, i // 2, i % 2, 0, 0, 0)),
        out_shape=jax.ShapeDtypeStruct((CORE, X, ZL, ZH, MODES, 128), jnp.float32),
        scratch_shapes=[pltpu.VMEM((rows, 1024), jnp.float32)],
        compiler_params=params(),
        cost_estimate=pl.CostEstimate(flops=16 * 2**20, bytes_accessed=2 * 2**20, transcendentals=2**18),
        name="prefix_state",
    )(lag, prefix_input, rates_t)


def attend_kernel(q_ref, kv_ref, o_ref, lse_ref, s_scr, m_scr):
    step = pl.program_id(0)
    tiles = pl.num_programs(0) - 1
    key_rows = kv_ref.shape[2]
    per_span = SPAN // key_rows
    spans = kv_ref.shape[0] // per_span

    def run(do_scores, do_values):
        if do_scores:
            slot = lax.rem(step, 2)
            query = q_ref[...]
            best = None
        if do_values:
            old = lax.rem(step + 1, 2)
            top = jnp.concatenate([m_scr[old]] * (SPAN // 128), axis=1)
            total = jnp.zeros((TILE, 128), jnp.float32)
            acc = jnp.zeros((TILE, HD), jnp.float32)
        for j in range(spans):
            cols = slice(j * SPAN, (j + 1) * SPAN)
            if do_scores:
                keys = kv_ref[j * per_span : (j + 1) * per_span, 0].reshape(SPAN, HD)
                scores = dot_t(query, keys)
                s_scr[slot, :, cols] = scores
                for k in range(SPAN // 128):
                    part = scores[:, k * 128 : (k + 1) * 128]
                    best = part if best is None else jnp.maximum(best, part)
            if do_values:
                weights = jnp.exp2(s_scr[old, :, cols] * SCALE2 - top)
                for k in range(SPAN // 128):
                    total = total + weights[:, k * 128 : (k + 1) * 128]
                values = kv_ref[j * per_span : (j + 1) * per_span, 1].reshape(SPAN, HD)
                acc = acc + jnp.dot(
                    weights.astype(jnp.bfloat16), values, preferred_element_type=jnp.float32
                )
        if do_scores:
            row_best = jnp.max(best, axis=1, keepdims=True) * SCALE2
            m_scr[slot] = jnp.broadcast_to(row_best, (TILE, 128))
        if do_values:
            denom = jnp.sum(total, axis=1, keepdims=True)
            o_ref[...] = (acc / denom).astype(o_ref.dtype)
            lse = m_scr[old] + jnp.log2(jnp.broadcast_to(denom, (TILE, 128)))
            lse_ref[...] = lse.T[:8, :]

    @pl.when(step == 0)
    def _():
        run(True, False)

    @pl.when((step > 0) & (step < tiles))
    def _():
        run(True, True)

    @pl.when(step == tiles)
    def _():
        run(False, True)


def attend(q, kv, dtype):
    tiles = ROWS // TILE
    keys = kv.shape[0] * kv.shape[2]
    return pl.pallas_call(
        attend_kernel,
        grid=(tiles + 1,),
        in_specs=[
            pl.BlockSpec((TILE, HD), lambda i: (jnp.minimum(i, tiles - 1), 0)),
            pl.BlockSpec(kv.shape, lambda i: (0, 0, 0, 0), pipeline_mode=pl.Buffered(1)),
        ],
        out_specs=[
            pl.BlockSpec((TILE, HD), lambda i: (jnp.maximum(i - 1, 0), 0)),
            pl.BlockSpec((8, TILE), lambda i: (0, jnp.maximum(i - 1, 0))),
        ],
        out_shape=[
            jax.ShapeDtypeStruct((ROWS, HD), dtype),
            jax.ShapeDtypeStruct((8, ROWS), jnp.float32),
        ],
        scratch_shapes=[
            pltpu.VMEM((2, TILE, keys), jnp.float32),
            pltpu.VMEM((2, TILE, 128), jnp.float32),
        ],
        compiler_params=params(),
        cost_estimate=pl.CostEstimate(
            flops=4 * ROWS * keys * HD, bytes_accessed=3 * 2**20, transcendentals=ROWS * keys
        ),
        name="attend",
    )(q, kv)


def own_kernel(attn_ref, o_ref, lse_ref):
    for v in range(VPD):
        for i in range(S // TILE):
            rows = slice(i * TILE, (i + 1) * TILE)
            seen = (i + 1) * TILE
            scores = dot_t(attn_ref[0, v, rows], attn_ref[1, v, :seen]) * SCALE2
            q_pos = lax.broadcasted_iota(jnp.int32, (TILE, seen), 0) + i * TILE
            k_pos = lax.broadcasted_iota(jnp.int32, (TILE, seen), 1)
            scores = jnp.where(q_pos >= k_pos, scores, -jnp.inf)
            top = jnp.max(scores, axis=1, keepdims=True)
            weights = jnp.exp2(scores - top)
            denom = jnp.sum(weights, axis=1, keepdims=True)
            acc = jnp.dot(
                weights.astype(jnp.bfloat16), attn_ref[2, v, :seen], preferred_element_type=jnp.float32
            )
            out = slice(v * S + i * TILE, v * S + (i + 1) * TILE)
            o_ref[out] = acc / denom
            lse = jnp.broadcast_to(top + jnp.log2(denom), (TILE, 128))
            lse_ref[:, out] = lse.T[:8, :]


def own_attention(suffix_attn):
    return pl.pallas_call(
        own_kernel,
        out_shape=[
            jax.ShapeDtypeStruct((ROWS, HD), jnp.float32),
            jax.ShapeDtypeStruct((8, ROWS), jnp.float32),
        ],
        compiler_params=params(),
        cost_estimate=pl.CostEstimate(flops=2**28, bytes_accessed=2 * 2**20, transcendentals=2**19),
        name="own_attention",
    )(suffix_attn)


def conv_kernel(hyena_ref, resid_ref, rate_ref, amp_ref, state_ref, base_ref, x32, y32):
    chunks = S // CHUNK
    lanes = VPD * chunks
    for v in range(VPD):
        x32[v * S : (v + 1) * S] = hyena_ref[1, v].astype(jnp.float32)
    decay, far = [], []
    for m in range(MODES):
        rate = jnp.broadcast_to(rate_ref[m : m + 1, :], (lanes, 128))
        decay.append(jnp.exp(-rate))
        far.append(jnp.exp(-rate * CHUNK))

    def first_pass(i, states):
        x = x32[pl.ds(i, lanes, stride=CHUNK), :]
        return tuple(s * d + x for s, d in zip(states, decay))

    zero = jnp.zeros((lanes, 128), jnp.float32)
    ends = lax.fori_loop(0, CHUNK, first_pass, (zero,) * MODES, unroll=8)
    chunk = lax.broadcasted_iota(jnp.int32, (lanes, 128), 0) % chunks
    starts = []
    for m in range(MODES):
        carried = jnp.broadcast_to(state_ref[m : m + 1, :], (lanes, 128))
        for step in range(1, chunks):
            moved = pltpu.roll(carried * far[m] + ends[m], 1, axis=0)
            carried = jnp.where(chunk == step, moved, carried)
        starts.append(carried)

    amps = [jnp.broadcast_to(amp_ref[m : m + 1, :], (lanes, 128)) for m in range(MODES)]

    def second_pass(i, states):
        x = x32[pl.ds(i, lanes, stride=CHUNK), :]
        states = tuple(s * d + x for s, d in zip(states, decay))
        terms = [s * a for s, a in zip(states, amps)]
        while len(terms) > 1:
            terms = [a + b for a, b in zip(terms[::2], terms[1::2])]
        y32[pl.ds(i, lanes, stride=CHUNK), :] = terms[0]
        return states

    lax.fori_loop(0, CHUNK, second_pass, tuple(starts), unroll=8)
    for v in range(VPD):
        rows = slice(v * S, (v + 1) * S)
        base_ref[rows] = resid_ref[v].astype(jnp.float32) + hyena_ref[0, v].astype(jnp.float32) * y32[rows]


def conv_base(suffix_hyena, suffix_resid, rates, amps, state):
    return pl.pallas_call(
        conv_kernel,
        out_shape=jax.ShapeDtypeStruct((ROWS, HD), jnp.float32),
        scratch_shapes=[pltpu.VMEM((ROWS, HD), jnp.float32), pltpu.VMEM((ROWS, HD), jnp.float32)],
        compiler_params=params(),
        cost_estimate=pl.CostEstimate(flops=2**25, bytes_accessed=2 * 2**20, transcendentals=2**15),
        name="suffix_conv",
    )(suffix_hyena, suffix_resid, rates, amps, state)


def combine_kernel(*refs):
    base_ref, gain_ref = refs[:2]
    parts = refs[2:-2]
    out_ref, hid = refs[-2:]
    outs, lses = parts[::2], parts[1::2]
    for i in range(ROWS // TILE):
        rows = slice(i * TILE, (i + 1) * TILE)
        cols = [ref[:, rows] for ref in lses]
        top = functools.reduce(jnp.maximum, cols)
        shares = [jnp.exp2(c - top) for c in cols]
        whole = functools.reduce(jnp.add, shares)
        hidden = base_ref[rows]
        for share, ref in zip(shares, outs):
            factor = (share / whole).T[:, :1]
            hidden = hidden + factor * ref[rows].astype(jnp.float32)
        hid[rows] = hidden * gain_ref[...]
    for g in range(GROUPS):
        x, zl, core, zh = g // 16, g // 4 % 4, g // 2 % 2, g % 2
        pair = jnp.concatenate([hid[v * S + g * 8 : v * S + g * 8 + 8] for v in range(VPD)], axis=0)
        at = (zl * ZH + zh) * 16
        out_ref[core, x, at : at + 16] = pair.astype(jnp.bfloat16)


def combine(base, gain, parts):
    return pl.pallas_call(
        combine_kernel,
        out_shape=jax.ShapeDtypeStruct((CORE, X, 128, 128), jnp.bfloat16),
        scratch_shapes=[pltpu.VMEM((ROWS, HD), jnp.float32)],
        compiler_params=params(),
        cost_estimate=pl.CostEstimate(flops=2**22, bytes_accessed=3 * 2**20, transcendentals=2**14),
        name="combine",
    )(base, gain, *parts)


def logits_kernel(*refs):
    hids, reads, gains = refs[:X], refs[X : 2 * X], refs[2 * X : 3 * X]
    out_ref = refs[-1]
    logits = jnp.zeros((128, VOCAB), jnp.float32)
    squares = jnp.zeros((128, 128), jnp.float32)
    for hid, read, gain in zip(hids, reads, gains):
        for c in range(CORE):
            block = hid[c]
            logits = logits + jnp.dot(block, read[c], preferred_element_type=jnp.float32)
            plain = block.astype(jnp.float32) / gain[c : c + 1, :]
            squares = squares + plain * plain
    sums = jnp.broadcast_to(jnp.sum(squares, axis=1, keepdims=True), (128, 128))
    for k in range(Z):
        rows = slice(k * 16, (k + 1) * 16)
        z = k % ZH * ZL + k // ZH
        out_ref[z, :, :VOCAB] = logits[rows]
        out_ref[z, :, VOCAB:] = sums[rows]


def partial_logits(hids, reads, gains):
    return pl.pallas_call(
        logits_kernel,
        out_shape=jax.ShapeDtypeStruct((Z, 16, VOCAB + 128), jnp.float32),
        compiler_params=params(),
        cost_estimate=pl.CostEstimate(flops=2**27, bytes_accessed=2 * 2**20, transcendentals=0),
        name="partial_logits",
    )(*hids, *reads, *gains)


def final_kernel(group_ref, next_ref, pos_ref, mut_ref, *refs):
    out_ref = refs[-1]
    whole = functools.reduce(jnp.add, [ref[...] for ref in refs[:-1]])
    mean_square = whole[:, VOCAB : VOCAB + 1] * (1.0 / D)
    logits = whole[:, :VOCAB] * lax.rsqrt(mean_square + 1e-5)
    top = jnp.max(logits, axis=1, keepdims=True)
    log_sum = top + jnp.log(jnp.sum(jnp.exp(logits - top), axis=1, keepdims=True))
    row = lax.broadcasted_iota(jnp.int32, (8, VOCAB), 0)
    token = lax.broadcasted_iota(jnp.int32, (8, VOCAB), 1)
    following = jnp.zeros((8, VOCAB), jnp.int32)
    for r in range(8):
        following = jnp.where(row == r, next_ref[r], following)
    position = row + group_ref[0] * 8
    lane = lax.broadcasted_iota(jnp.int32, (8, VPD), 1)
    result = jnp.zeros((8, VPD), jnp.float32)
    for v in range(VPD):
        target = jnp.where(position == pos_ref[v], mut_ref[v], following)
        rows = slice(v * 8, v * 8 + 8)
        picked = jnp.sum(jnp.where(token == target, logits[rows], 0.0), axis=1, keepdims=True)
        result = jnp.where(lane == v, picked - log_sum[rows], result)
    out_ref[...] = result


def finish(group, ref_next, mutation_pos, mutation_base, parts):
    smem = pl.BlockSpec(memory_space=pltpu.SMEM)
    vmem = pl.BlockSpec(memory_space=pltpu.VMEM)
    return pl.pallas_call(
        final_kernel,
        in_specs=[smem] * 4 + [vmem] * len(parts),
        out_shape=jax.ShapeDtypeStruct((8, VPD), jnp.float32),
        compiler_params=params(),
        name="finish",
    )(group, ref_next, mutation_pos, mutation_base, *parts)


def ring(size, shift):
    return [(i, (i + shift) % size) for i in range(size)]


def z_ring(shift):
    index = lambda z: z % ZL * ZH + z // ZL
    return [(index(z), index((z + shift) % Z)) for z in range(Z)]


SWAP = [(0, 1), (1, 0)]


def pick(array, index):
    return lax.dynamic_index_in_dim(array, index, 0, keepdims=False)


def on_device(
    prefix_input,
    prefix_cache,
    decay_rates,
    residues,
    suffix_hyena,
    suffix_attn,
    suffix_resid,
    norm_gain,
    readout,
    ref_next,
    mutation_pos,
    mutation_base,
):
    x, zl, core = lax.axis_index("x"), lax.axis_index("zl"), lax.axis_index("core")
    y, zh = lax.axis_index("y"), lax.axis_index("zh")
    z = zh * ZL + zl
    group = ((x * ZL + zl) * CORE + core) * ZH + zh
    shard_rows = prefix_input.shape[0]
    key_shards = prefix_cache.reshape(2, shard_rows, GROUPS, HD).transpose(2, 0, 1, 3)
    kv = lax.all_to_all(key_shards, ("x", "zl", "core", "zh"), split_axis=0, concat_axis=0, tiled=True)

    queries = suffix_attn[0].reshape(ROWS, HD)
    others = [lax.ppermute(queries, "y", ring(Y, k)) for k in range(1, Y)]

    rates_t = decay_rates.T
    amps_t = residues.T
    first = (((x * ZL + zl) * CORE + core) * Y + y) * ZH + zh
    lag = shard_rows * (GROUPS * Y - 1 - first)
    states = local_states(lag.astype(jnp.int32).reshape(1), prefix_input, rates_t)
    states = pick(states, core) + lax.ppermute(pick(states, 1 - core), "core", SWAP)
    summed = pick(states, x)
    for k in range(1, X):
        summed = summed + lax.ppermute(pick(states, (x + k) % X), "x", ring(X, k))
    states = summed.reshape(Z, MODES, 128)
    summed = pick(states, zl * ZH + zh)
    for k in range(1, Z):
        to = (z + k) % Z
        summed = summed + lax.ppermute(pick(states, to % ZL * ZH + to // ZL), ("zl", "zh"), z_ring(k))
    state = summed
    for k in range(1, Y):
        state = state + lax.ppermute(summed, "y", ring(Y, k))

    own_rates = lax.dynamic_slice_in_dim(rates_t, group * 128, 128, 1)
    own_amps = lax.dynamic_slice_in_dim(amps_t, group * 128, 128, 1)
    base = conv_base(suffix_hyena, suffix_resid, own_rates, own_amps, state)
    own_out, own_lse = own_attention(suffix_attn)

    pair_read = jnp.stack([readout, lax.ppermute(readout, "core", SWAP)])
    gain = norm_gain.reshape(1, HD)
    pair_gain = jnp.concatenate([gain, lax.ppermute(gain, "core", SWAP)])
    reads = [pair_read] + [lax.ppermute(pair_read, "x", ring(X, k)) for k in range(1, X)]
    gains = [pair_gain] + [lax.ppermute(pair_gain, "x", ring(X, k)) for k in range(1, X)]

    parts = {}
    for k in (2, 1, 3):
        out, lse = attend(others[k - 1], kv, jnp.bfloat16)
        back = ring(Y, Y - k)
        parts[k] = (lax.ppermute(out, "y", back), lax.ppermute(lse, "y", back))
    parts[0] = attend(queries, kv, jnp.float32)
    flat = [own_out, own_lse]
    for k in range(Y):
        flat += parts[k]
    hidden = combine(base, gain, flat)

    mine, theirs = pick(hidden, core), lax.ppermute(pick(hidden, 1 - core), "core", SWAP)

    def pair_for(dest):
        return jnp.stack([pick(mine, dest), pick(theirs, dest)])

    hids = [pair_for(x)]
    for k in range(1, X):
        hids.append(lax.ppermute(pair_for((x + k) % X), "x", ring(X, k)))
    shares = partial_logits(hids, reads, gains)
    pieces = [pick(shares, z)]
    for k in range(1, Z):
        pieces.append(lax.ppermute(pick(shares, (z + k) % Z), ("zl", "zh"), z_ring(k)))
    return finish(group.astype(jnp.int32).reshape(1), ref_next, mutation_pos, mutation_base, pieces)


def solution(mesh):
    fine = Mesh(mesh.devices.reshape(X, ZL, CORE, Y, ZH), ("x", "zl", "core", "y", "zh"))
    seq, groups, every = ("x", "zl", "core"), ("x", "zl", "core", "zh"), ("x", "zl", "core", "y", "zh")
    return jax.shard_map(
        on_device,
        mesh=fine,
        in_specs=(
            P(every, None),
            P(None, every, None),
            P(),
            P(),
            P(None, "y", None, groups),
            P(None, "y", None, groups),
            P("y", None, groups),
            P(groups),
            P(groups, None),
            P(groups),
            P("y"),
            P("y"),
        ),
        out_specs=P(groups, "y"),
        check_vma=False,
    )
```

```python
import functools

import jax
import jax.numpy as jnp
from jax import lax
from jax.experimental import pallas as pl
from jax.experimental.pallas import tpu as pltpu
from jax.sharding import Mesh
from jax.sharding import PartitionSpec as P

D = 8192
HD = 128
MODES = 16
S = 512
LOG2E = 1.4426950408889634
SCALE2 = HD**-0.5 * LOG2E
X, ZL, CORE, Y, ZH = 4, 4, 2, 4, 2
Z = ZL * ZH
GROUPS = X * ZL * CORE * ZH
VPD = 2
ROWS = VPD * S
VOCAB = 512
TILE = 256
SPAN = 512
CHUNK = 128
STATS = 32
VMEM_LIMIT = 56 * 1024 * 1024


def params(**kw):
    return pltpu.CompilerParams(vmem_limit_bytes=VMEM_LIMIT, **kw)


def dot_t(a, b):
    return lax.dot_general(a, b, (((1,), (1,)), ((), ())), preferred_element_type=jnp.float32)


def state_kernel(lag_ref, x_ref, rate_ref, out_ref, x32):
    x32[...] = x_ref[...].astype(jnp.float32)
    rate = rate_ref[...]
    decay = jnp.exp(-rate)
    state = jnp.zeros_like(decay)
    for row in range(x_ref.shape[0]):
        state = state * decay + x32[row : row + 1, :]
    state = state * jnp.exp(-rate * lag_ref[0].astype(jnp.float32))
    for zl in range(2):
        for core in range(CORE):
            for zh in range(ZH):
                g = (zl * CORE + core) * ZH + zh
                out_ref[core, 0, zl, zh] = state[:, g * 128 : (g + 1) * 128]


def local_states(lag, prefix_input, rates_t):
    rows = prefix_input.shape[0]
    return pl.pallas_call(
        state_kernel,
        grid=(8,),
        in_specs=[
            pl.BlockSpec(memory_space=pltpu.SMEM),
            pl.BlockSpec((rows, 1024), lambda i: (0, i)),
            pl.BlockSpec((MODES, 1024), lambda i: (0, i)),
        ],
        out_specs=pl.BlockSpec((CORE, 1, 2, ZH, MODES, 128), lambda i: (0, i // 2, i % 2, 0, 0, 0)),
        out_shape=jax.ShapeDtypeStruct((CORE, X, ZL, ZH, MODES, 128), jnp.float32),
        scratch_shapes=[pltpu.VMEM((rows, 1024), jnp.float32)],
        compiler_params=params(),
        cost_estimate=pl.CostEstimate(flops=16 * 2**20, bytes_accessed=2 * 2**20, transcendentals=2**18),
        name="prefix_state",
    )(lag, prefix_input, rates_t)


def diagonal():
    return lax.broadcasted_iota(jnp.int32, (128, 128), 0) == lax.broadcasted_iota(jnp.int32, (128, 128), 1)


def split_terms(left):
    terms = []
    for _ in range(3):
        term = left.astype(jnp.bfloat16).astype(jnp.float32)
        terms.append(term)
        left = left - term
    return terms


def stats_block(lse):
    same = diagonal()
    lines = [
        jnp.sum(jnp.where(same, lse[i * 128 : (i + 1) * 128], 0.0), axis=0, keepdims=True)
        for i in range(ROWS // 128)
    ]
    terms = split_terms(jnp.concatenate(lines, axis=0))
    return jnp.concatenate(terms + [jnp.zeros_like(terms[0])], axis=0).astype(jnp.bfloat16)


def attend_kernel(q_ref, kv_ref, o_ref):
    query = q_ref[...]
    per_span = SPAN // kv_ref.shape[2]
    best = None
    for j in range(kv_ref.shape[0] // per_span):
        shards = slice(j * per_span, (j + 1) * per_span)
        scores = dot_t(query, kv_ref[shards, 0].reshape(SPAN, HD))
        values = kv_ref[shards, 1].reshape(SPAN, HD)
        top = jnp.max(scores, axis=1, keepdims=True) * SCALE2
        if best is not None:
            top = jnp.maximum(best, top)
        weights = jnp.exp2(scores * SCALE2 - top)
        part = jnp.sum(weights, axis=1, keepdims=True)
        value = jnp.dot(weights.astype(jnp.bfloat16), values, preferred_element_type=jnp.float32)
        if best is None:
            denom, acc = part, value
        else:
            factor = jnp.exp2(best - top)
            denom, acc = denom * factor + part, acc * factor + value
        best = top
    o_ref[:ROWS] = (acc / denom).astype(jnp.bfloat16)
    o_ref[ROWS:] = stats_block(best + jnp.log2(denom))


def attend(q, kv):
    keys = kv.shape[0] * kv.shape[2]
    return pl.pallas_call(
        attend_kernel,
        out_shape=jax.ShapeDtypeStruct((ROWS + STATS, HD), jnp.bfloat16),
        compiler_params=params(),
        cost_estimate=pl.CostEstimate(
            flops=8 * ROWS * keys * HD, bytes_accessed=3 * 2**20, transcendentals=ROWS * keys
        ),
        name="attend",
    )(q, kv)


def own_kernel(attn_ref, o_ref):
    lses = []
    for v in range(VPD):
        for i in range(S // TILE):
            rows = slice(i * TILE, (i + 1) * TILE)
            seen = (i + 1) * TILE
            scores = dot_t(attn_ref[0, v, rows], attn_ref[1, v, :seen]) * SCALE2
            q_pos = lax.broadcasted_iota(jnp.int32, (TILE, seen), 0) + i * TILE
            k_pos = lax.broadcasted_iota(jnp.int32, (TILE, seen), 1)
            scores = jnp.where(q_pos >= k_pos, scores, -jnp.inf)
            top = jnp.max(scores, axis=1, keepdims=True)
            weights = jnp.exp2(scores - top)
            denom = jnp.sum(weights, axis=1, keepdims=True)
            acc = jnp.dot(
                weights.astype(jnp.bfloat16), attn_ref[2, v, :seen], preferred_element_type=jnp.float32
            )
            out = slice(v * S + i * TILE, v * S + (i + 1) * TILE)
            o_ref[out] = (acc / denom).astype(jnp.bfloat16)
            lses.append(top + jnp.log2(denom))
    o_ref[ROWS:] = stats_block(jnp.concatenate(lses, axis=0))


def own_attention(suffix_attn):
    return pl.pallas_call(
        own_kernel,
        out_shape=jax.ShapeDtypeStruct((ROWS + STATS, HD), jnp.bfloat16),
        compiler_params=params(),
        cost_estimate=pl.CostEstimate(flops=2**28, bytes_accessed=2 * 2**20, transcendentals=2**19),
        name="own_attention",
    )(suffix_attn)


def conv_kernel(hyena_ref, resid_ref, rate_ref, amp_ref, base_ref, x32, y32):
    chunks = S // CHUNK
    lanes = VPD * chunks
    for v in range(VPD):
        x32[v * S : (v + 1) * S] = hyena_ref[1, v].astype(jnp.float32)
    decay, far = [], []
    for m in range(MODES):
        rate = jnp.broadcast_to(rate_ref[m : m + 1, :], (lanes, 128))
        decay.append(jnp.exp(-rate))
        far.append(jnp.exp(-rate * CHUNK))

    def first_pass(i, states):
        x = x32[pl.ds(i, lanes, stride=CHUNK), :]
        return tuple(s * d + x for s, d in zip(states, decay))

    zero = jnp.zeros((lanes, 128), jnp.float32)
    ends = lax.fori_loop(0, CHUNK, first_pass, (zero,) * MODES, unroll=8)
    chunk = lax.broadcasted_iota(jnp.int32, (lanes, 128), 0) % chunks
    starts = []
    for m in range(MODES):
        carried = zero
        for step in range(1, chunks):
            moved = pltpu.roll(carried * far[m] + ends[m], 1, axis=0)
            carried = jnp.where(chunk == step, moved, carried)
        starts.append(carried)

    amps = [jnp.broadcast_to(amp_ref[m : m + 1, :], (lanes, 128)) for m in range(MODES)]

    def second_pass(i, states):
        x = x32[pl.ds(i, lanes, stride=CHUNK), :]
        states = tuple(s * d + x for s, d in zip(states, decay))
        terms = [s * a for s, a in zip(states, amps)]
        while len(terms) > 1:
            terms = [a + b for a, b in zip(terms[::2], terms[1::2])]
        y32[pl.ds(i, lanes, stride=CHUNK), :] = terms[0]
        return states

    lax.fori_loop(0, CHUNK, second_pass, tuple(starts), unroll=8)
    for v in range(VPD):
        rows = slice(v * S, (v + 1) * S)
        base_ref[rows] = resid_ref[v].astype(jnp.float32) + hyena_ref[0, v].astype(jnp.float32) * y32[rows]


def conv_base(suffix_hyena, suffix_resid, rates, amps):
    return pl.pallas_call(
        conv_kernel,
        out_shape=jax.ShapeDtypeStruct((ROWS, HD), jnp.float32),
        scratch_shapes=[pltpu.VMEM((ROWS, HD), jnp.float32), pltpu.VMEM((ROWS, HD), jnp.float32)],
        compiler_params=params(),
        cost_estimate=pl.CostEstimate(flops=2**25, bytes_accessed=2 * 2**20, transcendentals=2**15),
        name="suffix_conv",
    )(suffix_hyena, suffix_resid, rates, amps)


def combine_kernel(base_ref, gain_ref, hyena_ref, rate_ref, amp_ref, state_ref, *refs):
    parts, out_ref, hid, squares, tail = refs[:-4], *refs[-4:]
    state = functools.reduce(jnp.add, [state_ref[k] for k in range(Z)])
    ahead = lax.broadcasted_iota(jnp.int32, (8, 128), 0).astype(jnp.float32) + 1.0
    terms, decay = [], []
    for m in range(MODES):
        rate = jnp.broadcast_to(rate_ref[m : m + 1, :], (8, 128))
        scale = amp_ref[m : m + 1, :] * state[m : m + 1, :]
        terms.append(scale * jnp.exp(-rate * ahead))
        decay.append(jnp.exp(-rate * 8.0))
    for k in range(S // 8):
        sums = terms
        while len(sums) > 1:
            sums = [p + q for p, q in zip(sums[::2], sums[1::2])]
        tail[k * 8 : k * 8 + 8] = sums[0]
        terms = [t * d for t, d in zip(terms, decay)]

    lses = []
    for ref in parts:
        stats = ref[ROWS:].astype(jnp.float32)
        lses.append(stats[:8] + stats[8:16] + stats[16:24])
    top = functools.reduce(jnp.maximum, lses)
    shares = [jnp.exp2(lse - top) for lse in lses]
    whole = functools.reduce(jnp.add, shares)
    factors = [(share / whole).T for share in shares]
    gain = gain_ref[...]
    for i in range(ROWS // 128):
        rows = slice(i * 128, (i + 1) * 128)
        v, at = i * 128 // S, i * 128 % S
        gate = hyena_ref[0, v, at : at + 128].astype(jnp.float32)
        hidden = base_ref[rows] + gate * tail[at : at + 128]
        for factor, ref in zip(factors, parts):
            hidden = hidden + factor[:, i : i + 1] * ref[rows].astype(jnp.float32)
        hid[rows] = hidden * gain
        squares[rows] = jnp.broadcast_to(jnp.sum(hidden * hidden, axis=1, keepdims=True), (128, 128))
    same = diagonal()
    for x in range(X):
        for core in range(CORE):
            columns = []
            for k in range(Z):
                g = ((x * ZL + k // ZH) * CORE + core) * ZH + k % ZH
                spots = [slice(v * S + g * 8, v * S + g * 8 + 8) for v in range(VPD)]
                pair = jnp.concatenate([hid[spot] for spot in spots], axis=0)
                out_ref[x * CORE + core, k * 16 : k * 16 + 16] = pair.astype(jnp.bfloat16)
                columns += [squares[spot] for spot in spots]
            line = jnp.sum(jnp.where(same, jnp.concatenate(columns, axis=0), 0.0), axis=0, keepdims=True)
            spare = jnp.zeros((13, 128), jnp.float32)
            rows = jnp.concatenate(split_terms(line) + [spare], axis=0)
            out_ref[x * CORE + core, 128:] = rows.astype(jnp.bfloat16)


def combine(base, gain, suffix_hyena, rates, amps, states, parts):
    whole = lambda a: pl.BlockSpec(a.shape, lambda i: (0,) * a.ndim)
    args = (base, gain, suffix_hyena, rates, amps, states, *parts)
    specs = [whole(a) for a in args]
    specs[2] = pl.BlockSpec((1, VPD, S, HD), lambda i: (0, 0, 0, 0))
    return pl.pallas_call(
        combine_kernel,
        grid=(1,),
        in_specs=specs,
        out_specs=pl.BlockSpec((X * CORE, 144, 128), lambda i: (0, 0, 0)),
        out_shape=jax.ShapeDtypeStruct((X * CORE, 144, 128), jnp.bfloat16),
        scratch_shapes=[pltpu.VMEM((rows, HD), jnp.float32) for rows in (ROWS, ROWS, S)],
        compiler_params=params(),
        cost_estimate=pl.CostEstimate(flops=2**22, bytes_accessed=3 * 2**20, transcendentals=2**14),
        name="combine",
    )(*args)


def logits_kernel(source_ref, hid_ref, *refs):
    reads, out_ref = refs[:-1], refs[-1]
    logits = jnp.zeros((128, VOCAB), jnp.float32)
    line = jnp.zeros((1, 128), jnp.float32)
    for k, ref in enumerate(reads):
        for c in range(CORE):
            block = hid_ref[source_ref[k * CORE + c]]
            logits = logits + jnp.dot(block[:128], ref[c], preferred_element_type=jnp.float32)
            line = line + jnp.sum(block[128:].astype(jnp.float32), axis=0, keepdims=True)
    sums = jnp.sum(jnp.where(diagonal(), line, 0.0), axis=1, keepdims=True)
    sums = jnp.broadcast_to(sums, (128, 128))
    high = sums.astype(jnp.bfloat16)
    low = (sums - high.astype(jnp.float32)).astype(jnp.bfloat16)
    for k in range(Z):
        rows = slice(k * 16, (k + 1) * 16)
        out_ref[k, :, :VOCAB] = logits[rows].astype(jnp.bfloat16)
        out_ref[k, :, VOCAB : VOCAB + 128] = high[rows]
        out_ref[k, :, VOCAB + 128 :] = low[rows]


def partial_logits(sources, hidden, reads):
    vmem = pl.BlockSpec(memory_space=pltpu.VMEM)
    return pl.pallas_call(
        logits_kernel,
        in_specs=[pl.BlockSpec(memory_space=pltpu.SMEM)] + [vmem] * (1 + len(reads)),
        out_shape=jax.ShapeDtypeStruct((Z, 16, VOCAB + 256), jnp.bfloat16),
        compiler_params=params(),
        cost_estimate=pl.CostEstimate(flops=2**27, bytes_accessed=2 * 2**20, transcendentals=0),
        name="partial_logits",
    )(sources, hidden, *reads)


def final_kernel(group_ref, next_ref, pos_ref, mut_ref, share_ref, out_ref):
    whole = jnp.zeros((16, VOCAB + 256), jnp.float32)
    for k in range(Z):
        whole = whole + share_ref[k].astype(jnp.float32)
    square_sum = whole[:, VOCAB : VOCAB + 1] + whole[:, VOCAB + 128 : VOCAB + 129]
    logits = whole[:, :VOCAB] * lax.rsqrt(square_sum * (1.0 / D) + 1e-5)
    top = jnp.max(logits, axis=1, keepdims=True)
    log_sum = top + jnp.log(jnp.sum(jnp.exp(logits - top), axis=1, keepdims=True))
    row = lax.broadcasted_iota(jnp.int32, (8, VOCAB), 0)
    token = lax.broadcasted_iota(jnp.int32, (8, VOCAB), 1)
    following = jnp.zeros((8, VOCAB), jnp.int32)
    for r in range(8):
        following = jnp.where(row == r, next_ref[r], following)
    position = row + group_ref[0] * 8
    here = lax.broadcasted_iota(jnp.int32, (8, 128), 0) == lax.broadcasted_iota(jnp.int32, (8, 128), 1)
    for v in range(VPD):
        target = jnp.where(position == pos_ref[v], mut_ref[v], following)
        rows = slice(v * 8, v * 8 + 8)
        picked = jnp.sum(jnp.where(token == target, logits[rows], 0.0), axis=1, keepdims=True)
        line = jnp.sum(jnp.where(here, picked - log_sum[rows], 0.0), axis=0, keepdims=True)
        out_ref[v : v + 1, :] = line[:, :8]


def finish(group, ref_next, mutation_pos, mutation_base, shares):
    smem = pl.BlockSpec(memory_space=pltpu.SMEM)
    return pl.pallas_call(
        final_kernel,
        in_specs=[smem] * 4 + [pl.BlockSpec(memory_space=pltpu.VMEM)],
        out_shape=jax.ShapeDtypeStruct((VPD, 8), jnp.float32),
        compiler_params=params(),
        name="finish",
    )(group, ref_next, mutation_pos, mutation_base, shares)


def ring(size, shift):
    return [(i, (i + shift) % size) for i in range(size)]


def paired(size, bit):
    return [(i, i ^ bit) for i in range(size)]


def pick(array, index, axis=0):
    return lax.dynamic_index_in_dim(array, index, axis, keepdims=False)


def halve(states, bit, partner, axis_name, axis, meanwhile=None):
    got = lax.ppermute(pick(states, 1 - bit, axis), axis_name, partner)
    if meanwhile is None:
        return pick(states, bit, axis) + got
    got, other = lax.optimization_barrier((got, meanwhile(states)))
    return pick(states, bit, axis) + got, other


def after(value, first):
    return lax.optimization_barrier((value, first))[0]


def on_device(
    prefix_input,
    prefix_cache,
    decay_rates,
    residues,
    suffix_hyena,
    suffix_attn,
    suffix_resid,
    norm_gain,
    readout,
    ref_next,
    mutation_pos,
    mutation_base,
):
    x, zl, core = lax.axis_index("x"), lax.axis_index("zl"), lax.axis_index("core")
    y, zh = lax.axis_index("y"), lax.axis_index("zh")
    group = ((x * ZL + zl) * CORE + core) * ZH + zh
    shard_rows = prefix_input.shape[0]
    key_shards = prefix_cache.reshape(2, shard_rows, GROUPS, HD).transpose(2, 0, 1, 3)
    kv = lax.all_to_all(key_shards, ("x", "zl", "core", "zh"), split_axis=0, concat_axis=0, tiled=True)

    queries = suffix_attn[0].reshape(ROWS, HD)
    others = [lax.ppermute(queries, "y", ring(Y, k)) for k in range(1, Y)]

    rates_t = decay_rates.T
    amps_t = residues.T
    first = (((x * ZL + zl) * CORE + core) * Y + y) * ZH + zh
    lag = shard_rows * (GROUPS * Y - 1 - first)
    states = local_states(lag.astype(jnp.int32).reshape(1), prefix_input, rates_t)
    own_rates = lax.dynamic_slice_in_dim(rates_t, group * 128, 128, 1)
    own_amps = lax.dynamic_slice_in_dim(amps_t, group * 128, 128, 1)
    state = halve(states, core, paired(CORE, 1), "core", 0)
    state = state.reshape(2, 2, Z, MODES, 128)
    state, own = halve(
        state, x % 2, paired(X, 1), "x", 1, lambda s: own_attention(after(suffix_attn, s))
    )
    state, base = halve(
        state,
        x // 2,
        paired(X, 2),
        "x",
        0,
        lambda s: conv_base(after(suffix_hyena, (s, others)), suffix_resid, own_rates, own_amps),
    )
    for bit in (1, 2):
        state = state + lax.ppermute(state, "y", paired(Y, bit))

    gain = norm_gain.reshape(1, HD)
    near = jnp.stack([readout, lax.ppermute(readout, "core", paired(CORE, 1))])
    reads = [near] + [lax.ppermute(near, "x", ring(X, k)) for k in range(1, X)]
    kv, reads, base, own, others, state = lax.optimization_barrier(
        (kv, reads, base, own, others, state)
    )
    states = lax.all_to_all(state, ("zl", "zh"), split_axis=0, concat_axis=0, tiled=True)

    parts = [own]
    for k in (2, 1, 3):
        parts.append(lax.ppermute(attend(others[k - 1], kv), "y", ring(Y, Y - k)))
    parts.append(attend(queries, kv))
    hidden = combine(base, gain, suffix_hyena, own_rates, own_amps, states, parts)
    hidden = lax.all_to_all(hidden, ("x", "core"), split_axis=0, concat_axis=0, tiled=True)
    sources = [(x + X - k) % X * CORE + (core if c == 0 else 1 - core) for k in range(X) for c in range(CORE)]
    shares = partial_logits(jnp.stack(sources).astype(jnp.int32), hidden, reads)
    shares = lax.all_to_all(shares, ("zl", "zh"), split_axis=0, concat_axis=0, tiled=True)
    group_id = group.astype(jnp.int32).reshape(1)
    return finish(group_id, ref_next, mutation_pos, mutation_base, shares).T


def solution(mesh):
    fine = Mesh(mesh.devices.reshape(X, ZL, CORE, Y, ZH), ("x", "zl", "core", "y", "zh"))
    seq, groups, every = ("x", "zl", "core"), ("x", "zl", "core", "zh"), ("x", "zl", "core", "y", "zh")
    return jax.shard_map(
        on_device,
        mesh=fine,
        in_specs=(
            P(every, None),
            P(None, every, None),
            P(),
            P(),
            P(None, "y", None, groups),
            P(None, "y", None, groups),
            P("y", None, groups),
            P(groups),
            P(groups, None),
            P(groups),
            P("y"),
            P("y"),
        ),
        out_specs=P(groups, "y"),
        check_vma=False,
    )
```

```python
import functools

import jax
import jax.numpy as jnp
from jax import lax
from jax.experimental import pallas as pl
from jax.experimental.pallas import tpu as pltpu
from jax.sharding import Mesh
from jax.sharding import PartitionSpec as P

D = 8192
HD = 128
MODES = 16
S = 512
LOG2E = 1.4426950408889634
SCALE2 = HD**-0.5 * LOG2E
X, ZL, CORE, Y, ZH = 4, 4, 2, 4, 2
Z = ZL * ZH
GROUPS = X * ZL * CORE * ZH
VPD = 2
ROWS = VPD * S
VOCAB = 512
TILE = 256
SPAN = 1024
CHUNK = 128
STATS = 32
VMEM_LIMIT = 56 * 1024 * 1024


def params(**kw):
    return pltpu.CompilerParams(vmem_limit_bytes=VMEM_LIMIT, **kw)


def dot_t(a, b):
    return lax.dot_general(a, b, (((1,), (1,)), ((), ())), preferred_element_type=jnp.float32)


def state_kernel(lag_ref, x_ref, rate_ref, out_ref, x32):
    x32[...] = x_ref[...].astype(jnp.float32)
    rate = rate_ref[...]
    decay = jnp.exp(-rate)
    state = jnp.zeros_like(decay)
    for row in range(x_ref.shape[0]):
        state = state * decay + x32[row : row + 1, :]
    state = state * jnp.exp(-rate * lag_ref[0].astype(jnp.float32))
    for zl in range(2):
        for core in range(CORE):
            for zh in range(ZH):
                g = (zl * CORE + core) * ZH + zh
                out_ref[core, 0, zl, zh] = state[:, g * 128 : (g + 1) * 128]


def local_states(lag, prefix_input, rates_t):
    rows = prefix_input.shape[0]
    return pl.pallas_call(
        state_kernel,
        grid=(8,),
        in_specs=[
            pl.BlockSpec(memory_space=pltpu.SMEM),
            pl.BlockSpec((rows, 1024), lambda i: (0, i)),
            pl.BlockSpec((MODES, 1024), lambda i: (0, i)),
        ],
        out_specs=pl.BlockSpec((CORE, 1, 2, ZH, MODES, 128), lambda i: (0, i // 2, i % 2, 0, 0, 0)),
        out_shape=jax.ShapeDtypeStruct((CORE, X, ZL, ZH, MODES, 128), jnp.float32),
        scratch_shapes=[pltpu.VMEM((rows, 1024), jnp.float32)],
        compiler_params=params(),
        cost_estimate=pl.CostEstimate(flops=16 * 2**20, bytes_accessed=2 * 2**20, transcendentals=2**18),
        name="prefix_state",
    )(lag, prefix_input, rates_t)


def diagonal():
    return lax.broadcasted_iota(jnp.int32, (128, 128), 0) == lax.broadcasted_iota(jnp.int32, (128, 128), 1)


def split_terms(left):
    terms = []
    for _ in range(3):
        term = left.astype(jnp.bfloat16).astype(jnp.float32)
        terms.append(term)
        left = left - term
    return terms


def stats_block(lse):
    same = diagonal()
    lines = [
        jnp.sum(jnp.where(same, lse[i * 128 : (i + 1) * 128], 0.0), axis=0, keepdims=True)
        for i in range(ROWS // 128)
    ]
    terms = split_terms(jnp.concatenate(lines, axis=0))
    return jnp.concatenate(terms + [jnp.zeros_like(terms[0])], axis=0).astype(jnp.bfloat16)


def attend_kernel(*refs):
    count = (len(refs) - 1) // 2
    queries, kv_ref, outs = refs[:count], refs[count], refs[count + 1 :]
    per_span = SPAN // kv_ref.shape[2]
    running = [None] * count
    for j in range(kv_ref.shape[0] // per_span):
        shards = slice(j * per_span, (j + 1) * per_span)
        keys = kv_ref[shards, 0].reshape(SPAN, HD)
        values = kv_ref[shards, 1].reshape(SPAN, HD)
        for i in range(count):
            scores = dot_t(queries[i][...], keys)
            top = jnp.max(scores, axis=1, keepdims=True) * SCALE2
            if j > 0:
                best, denom, acc = running[i]
                top = jnp.maximum(best, top)
            weights = jnp.exp2(scores * SCALE2 - top)
            part = jnp.sum(weights, axis=1, keepdims=True)
            value = jnp.dot(weights.astype(jnp.bfloat16), values, preferred_element_type=jnp.float32)
            if j > 0:
                factor = jnp.exp2(best - top)
                part, value = denom * factor + part, acc * factor + value
            running[i] = (top, part, value)
    for out_ref, (best, denom, acc) in zip(outs, running):
        out_ref[:ROWS] = (acc / denom).astype(jnp.bfloat16)
        out_ref[ROWS:] = stats_block(best + jnp.log2(denom))


def attend(queries, kv):
    keys = kv.shape[0] * kv.shape[2]
    count = len(queries)
    return pl.pallas_call(
        attend_kernel,
        out_shape=[jax.ShapeDtypeStruct((ROWS + STATS, HD), jnp.bfloat16)] * count,
        compiler_params=params(),
        cost_estimate=pl.CostEstimate(
            flops=8 * count * ROWS * keys * HD,
            bytes_accessed=3 * 2**20,
            transcendentals=count * ROWS * keys,
        ),
        name="attend",
    )(*queries, kv)


def own_kernel(attn_ref, o_ref):
    lses = []
    for v in range(VPD):
        for i in range(S // TILE):
            rows = slice(i * TILE, (i + 1) * TILE)
            seen = (i + 1) * TILE
            scores = dot_t(attn_ref[0, v, rows], attn_ref[1, v, :seen]) * SCALE2
            q_pos = lax.broadcasted_iota(jnp.int32, (TILE, seen), 0) + i * TILE
            k_pos = lax.broadcasted_iota(jnp.int32, (TILE, seen), 1)
            scores = jnp.where(q_pos >= k_pos, scores, -jnp.inf)
            top = jnp.max(scores, axis=1, keepdims=True)
            weights = jnp.exp2(scores - top)
            denom = jnp.sum(weights, axis=1, keepdims=True)
            acc = jnp.dot(
                weights.astype(jnp.bfloat16), attn_ref[2, v, :seen], preferred_element_type=jnp.float32
            )
            out = slice(v * S + i * TILE, v * S + (i + 1) * TILE)
            o_ref[out] = (acc / denom).astype(jnp.bfloat16)
            lses.append(top + jnp.log2(denom))
    o_ref[ROWS:] = stats_block(jnp.concatenate(lses, axis=0))


def own_attention(suffix_attn):
    return pl.pallas_call(
        own_kernel,
        out_shape=jax.ShapeDtypeStruct((ROWS + STATS, HD), jnp.bfloat16),
        compiler_params=params(),
        cost_estimate=pl.CostEstimate(flops=2**28, bytes_accessed=2 * 2**20, transcendentals=2**19),
        name="own_attention",
    )(suffix_attn)


def conv_kernel(hyena_ref, resid_ref, rate_ref, amp_ref, base_ref, x32, y32):
    chunks = S // CHUNK
    lanes = VPD * chunks
    for v in range(VPD):
        x32[v * S : (v + 1) * S] = hyena_ref[1, v].astype(jnp.float32)
    decay, far = [], []
    for m in range(MODES):
        rate = jnp.broadcast_to(rate_ref[m : m + 1, :], (lanes, 128))
        decay.append(jnp.exp(-rate))
        far.append(jnp.exp(-rate * CHUNK))

    def first_pass(i, states):
        x = x32[pl.ds(i, lanes, stride=CHUNK), :]
        return tuple(s * d + x for s, d in zip(states, decay))

    zero = jnp.zeros((lanes, 128), jnp.float32)
    ends = lax.fori_loop(0, CHUNK, first_pass, (zero,) * MODES, unroll=8)
    chunk = lax.broadcasted_iota(jnp.int32, (lanes, 128), 0) % chunks
    starts = []
    for m in range(MODES):
        carried = zero
        for step in range(1, chunks):
            moved = pltpu.roll(carried * far[m] + ends[m], 1, axis=0)
            carried = jnp.where(chunk == step, moved, carried)
        starts.append(carried)

    amps = [jnp.broadcast_to(amp_ref[m : m + 1, :], (lanes, 128)) for m in range(MODES)]

    def second_pass(i, states):
        x = x32[pl.ds(i, lanes, stride=CHUNK), :]
        states = tuple(s * d + x for s, d in zip(states, decay))
        terms = [s * a for s, a in zip(states, amps)]
        while len(terms) > 1:
            terms = [a + b for a, b in zip(terms[::2], terms[1::2])]
        y32[pl.ds(i, lanes, stride=CHUNK), :] = terms[0]
        return states

    lax.fori_loop(0, CHUNK, second_pass, tuple(starts), unroll=8)
    for v in range(VPD):
        rows = slice(v * S, (v + 1) * S)
        base_ref[rows] = resid_ref[v].astype(jnp.float32) + hyena_ref[0, v].astype(jnp.float32) * y32[rows]


def conv_base(suffix_hyena, suffix_resid, rates, amps):
    return pl.pallas_call(
        conv_kernel,
        out_shape=jax.ShapeDtypeStruct((ROWS, HD), jnp.float32),
        scratch_shapes=[pltpu.VMEM((ROWS, HD), jnp.float32), pltpu.VMEM((ROWS, HD), jnp.float32)],
        compiler_params=params(),
        cost_estimate=pl.CostEstimate(flops=2**25, bytes_accessed=2 * 2**20, transcendentals=2**15),
        name="suffix_conv",
    )(suffix_hyena, suffix_resid, rates, amps)


def combine_kernel(base_ref, gain_ref, hyena_ref, rate_ref, amp_ref, state_ref, *refs):
    parts, out_ref, hid, squares, tail = refs[:-4], *refs[-4:]
    state = functools.reduce(jnp.add, [state_ref[k] for k in range(Z)])
    ahead = lax.broadcasted_iota(jnp.int32, (8, 128), 0).astype(jnp.float32) + 1.0
    terms, decay = [], []
    for m in range(MODES):
        rate = jnp.broadcast_to(rate_ref[m : m + 1, :], (8, 128))
        scale = amp_ref[m : m + 1, :] * state[m : m + 1, :]
        terms.append(scale * jnp.exp(-rate * ahead))
        decay.append(jnp.exp(-rate * 8.0))
    for k in range(S // 8):
        sums = terms
        while len(sums) > 1:
            sums = [p + q for p, q in zip(sums[::2], sums[1::2])]
        tail[k * 8 : k * 8 + 8] = sums[0]
        terms = [t * d for t, d in zip(terms, decay)]

    lses = []
    for ref in parts:
        stats = ref[ROWS:].astype(jnp.float32)
        lses.append(stats[:8] + stats[8:16] + stats[16:24])
    top = functools.reduce(jnp.maximum, lses)
    shares = [jnp.exp2(lse - top) for lse in lses]
    whole = functools.reduce(jnp.add, shares)
    factors = [(share / whole).T for share in shares]
    gain = gain_ref[...]
    for i in range(ROWS // 128):
        rows = slice(i * 128, (i + 1) * 128)
        v, at = i * 128 // S, i * 128 % S
        gate = hyena_ref[0, v, at : at + 128].astype(jnp.float32)
        hidden = base_ref[rows] + gate * tail[at : at + 128]
        for factor, ref in zip(factors, parts):
            hidden = hidden + factor[:, i : i + 1] * ref[rows].astype(jnp.float32)
        hid[rows] = hidden * gain
        squares[rows] = jnp.broadcast_to(jnp.sum(hidden * hidden, axis=1, keepdims=True), (128, 128))
    same = diagonal()
    for x in range(X):
        for core in range(CORE):
            columns = []
            for k in range(Z):
                g = ((x * ZL + k // ZH) * CORE + core) * ZH + k % ZH
                spots = [slice(v * S + g * 8, v * S + g * 8 + 8) for v in range(VPD)]
                pair = jnp.concatenate([hid[spot] for spot in spots], axis=0)
                out_ref[x * CORE + core, k * 16 : k * 16 + 16] = pair.astype(jnp.bfloat16)
                columns += [squares[spot] for spot in spots]
            line = jnp.sum(jnp.where(same, jnp.concatenate(columns, axis=0), 0.0), axis=0, keepdims=True)
            spare = jnp.zeros((13, 128), jnp.float32)
            rows = jnp.concatenate(split_terms(line) + [spare], axis=0)
            out_ref[x * CORE + core, 128:] = rows.astype(jnp.bfloat16)


def combine(base, gain, suffix_hyena, rates, amps, states, parts):
    whole = lambda a: pl.BlockSpec(a.shape, lambda i: (0,) * a.ndim)
    args = (base, gain, suffix_hyena, rates, amps, states, *parts)
    specs = [whole(a) for a in args]
    specs[2] = pl.BlockSpec((1, VPD, S, HD), lambda i: (0, 0, 0, 0))
    return pl.pallas_call(
        combine_kernel,
        grid=(1,),
        in_specs=specs,
        out_specs=pl.BlockSpec((X * CORE, 144, 128), lambda i: (0, 0, 0)),
        out_shape=jax.ShapeDtypeStruct((X * CORE, 144, 128), jnp.bfloat16),
        scratch_shapes=[pltpu.VMEM((rows, HD), jnp.float32) for rows in (ROWS, ROWS, S)],
        compiler_params=params(),
        cost_estimate=pl.CostEstimate(flops=2**22, bytes_accessed=3 * 2**20, transcendentals=2**14),
        name="combine",
    )(*args)


def logits_kernel(source_ref, hid_ref, *refs):
    reads, out_ref = refs[:-1], refs[-1]
    logits = jnp.zeros((128, VOCAB), jnp.float32)
    line = jnp.zeros((1, 128), jnp.float32)
    for k, ref in enumerate(reads):
        for c in range(CORE):
            block = hid_ref[source_ref[k * CORE + c]]
            logits = logits + jnp.dot(block[:128], ref[c], preferred_element_type=jnp.float32)
            line = line + jnp.sum(block[128:].astype(jnp.float32), axis=0, keepdims=True)
    sums = jnp.sum(jnp.where(diagonal(), line, 0.0), axis=1, keepdims=True)
    sums = jnp.broadcast_to(sums, (128, 128))
    high = sums.astype(jnp.bfloat16)
    low = (sums - high.astype(jnp.float32)).astype(jnp.bfloat16)
    for k in range(Z):
        rows = slice(k * 16, (k + 1) * 16)
        out_ref[k, :, :VOCAB] = logits[rows].astype(jnp.bfloat16)
        out_ref[k, :, VOCAB : VOCAB + 128] = high[rows]
        out_ref[k, :, VOCAB + 128 :] = low[rows]


def partial_logits(sources, hidden, reads):
    vmem = pl.BlockSpec(memory_space=pltpu.VMEM)
    return pl.pallas_call(
        logits_kernel,
        in_specs=[pl.BlockSpec(memory_space=pltpu.SMEM)] + [vmem] * (1 + len(reads)),
        out_shape=jax.ShapeDtypeStruct((Z, 16, VOCAB + 256), jnp.bfloat16),
        compiler_params=params(),
        cost_estimate=pl.CostEstimate(flops=2**27, bytes_accessed=2 * 2**20, transcendentals=0),
        name="partial_logits",
    )(sources, hidden, *reads)


def final_kernel(group_ref, next_ref, pos_ref, mut_ref, share_ref, out_ref):
    whole = jnp.zeros((16, VOCAB + 256), jnp.float32)
    for k in range(Z):
        whole = whole + share_ref[k].astype(jnp.float32)
    square_sum = whole[:, VOCAB : VOCAB + 1] + whole[:, VOCAB + 128 : VOCAB + 129]
    logits = whole[:, :VOCAB] * lax.rsqrt(square_sum * (1.0 / D) + 1e-5)
    top = jnp.max(logits, axis=1, keepdims=True)
    log_sum = top + jnp.log(jnp.sum(jnp.exp(logits - top), axis=1, keepdims=True))
    row = lax.broadcasted_iota(jnp.int32, (8, VOCAB), 0)
    token = lax.broadcasted_iota(jnp.int32, (8, VOCAB), 1)
    following = jnp.zeros((8, VOCAB), jnp.int32)
    for r in range(8):
        following = jnp.where(row == r, next_ref[r], following)
    position = row + group_ref[0] * 8
    here = lax.broadcasted_iota(jnp.int32, (8, 128), 0) == lax.broadcasted_iota(jnp.int32, (8, 128), 1)
    for v in range(VPD):
        target = jnp.where(position == pos_ref[v], mut_ref[v], following)
        rows = slice(v * 8, v * 8 + 8)
        picked = jnp.sum(jnp.where(token == target, logits[rows], 0.0), axis=1, keepdims=True)
        line = jnp.sum(jnp.where(here, picked - log_sum[rows], 0.0), axis=0, keepdims=True)
        out_ref[v : v + 1, :] = line[:, :8]


def finish(group, ref_next, mutation_pos, mutation_base, shares):
    smem = pl.BlockSpec(memory_space=pltpu.SMEM)
    return pl.pallas_call(
        final_kernel,
        in_specs=[smem] * 4 + [pl.BlockSpec(memory_space=pltpu.VMEM)],
        out_shape=jax.ShapeDtypeStruct((VPD, 8), jnp.float32),
        compiler_params=params(),
        name="finish",
    )(group, ref_next, mutation_pos, mutation_base, shares)


def ring(size, shift):
    return [(i, (i + shift) % size) for i in range(size)]


def paired(size, bit):
    return [(i, i ^ bit) for i in range(size)]


def pick(array, index, axis=0):
    return lax.dynamic_index_in_dim(array, index, axis, keepdims=False)


def halve(states, bit, partner, axis_name, axis, meanwhile=None):
    got = lax.ppermute(pick(states, 1 - bit, axis), axis_name, partner)
    if meanwhile is None:
        return pick(states, bit, axis) + got
    got, other = lax.optimization_barrier((got, meanwhile(states)))
    return pick(states, bit, axis) + got, other


def after(value, first):
    return lax.optimization_barrier((value, first))[0]


def on_device(
    prefix_input,
    prefix_cache,
    decay_rates,
    residues,
    suffix_hyena,
    suffix_attn,
    suffix_resid,
    norm_gain,
    readout,
    ref_next,
    mutation_pos,
    mutation_base,
):
    x, zl, core = lax.axis_index("x"), lax.axis_index("zl"), lax.axis_index("core")
    y, zh = lax.axis_index("y"), lax.axis_index("zh")
    group = ((x * ZL + zl) * CORE + core) * ZH + zh
    shard_rows = prefix_input.shape[0]
    key_shards = prefix_cache.reshape(2, shard_rows, GROUPS, HD).transpose(2, 0, 1, 3)
    kv = lax.all_to_all(key_shards, ("x", "zl", "core", "zh"), split_axis=0, concat_axis=0, tiled=True)

    queries = suffix_attn[0].reshape(ROWS, HD)
    others = [lax.ppermute(queries, "y", ring(Y, k)) for k in range(1, Y)]

    rates_t = decay_rates.T
    amps_t = residues.T
    first = (((x * ZL + zl) * CORE + core) * Y + y) * ZH + zh
    lag = shard_rows * (GROUPS * Y - 1 - first)
    states = local_states(lag.astype(jnp.int32).reshape(1), prefix_input, rates_t)
    own_rates = lax.dynamic_slice_in_dim(rates_t, group * 128, 128, 1)
    own_amps = lax.dynamic_slice_in_dim(amps_t, group * 128, 128, 1)
    state = halve(states, core, paired(CORE, 1), "core", 0)
    state = state.reshape(2, 2, Z, MODES, 128)
    state, own = halve(
        state, x % 2, paired(X, 1), "x", 1, lambda s: own_attention(after(suffix_attn, s))
    )
    state, base = halve(
        state,
        x // 2,
        paired(X, 2),
        "x",
        0,
        lambda s: conv_base(after(suffix_hyena, (s, others)), suffix_resid, own_rates, own_amps),
    )
    for bit in (1, 2):
        state = state + lax.ppermute(state, "y", paired(Y, bit))

    gain = norm_gain.reshape(1, HD)
    near = jnp.stack([readout, lax.ppermute(readout, "core", paired(CORE, 1))])
    reads = [near] + [lax.ppermute(near, "x", ring(X, k)) for k in range(1, X)]
    kv, reads, base, own, others, state = lax.optimization_barrier(
        (kv, reads, base, own, others, state)
    )
    states = lax.all_to_all(state, ("zl", "zh"), split_axis=0, concat_axis=0, tiled=True)

    parts = [own]
    for shifts in ((2,), (1, 3)):
        for k, out in zip(shifts, attend([others[k - 1] for k in shifts], kv)):
            parts.append(lax.ppermute(out, "y", ring(Y, Y - k)))
    parts += attend([queries], kv)
    hidden = combine(base, gain, suffix_hyena, own_rates, own_amps, states, parts)
    hidden = lax.all_to_all(hidden, ("x", "core"), split_axis=0, concat_axis=0, tiled=True)
    sources = [(x + X - k) % X * CORE + (core if c == 0 else 1 - core) for k in range(X) for c in range(CORE)]
    shares = partial_logits(jnp.stack(sources).astype(jnp.int32), hidden, reads)
    shares = lax.all_to_all(shares, ("zl", "zh"), split_axis=0, concat_axis=0, tiled=True)
    group_id = group.astype(jnp.int32).reshape(1)
    return finish(group_id, ref_next, mutation_pos, mutation_base, shares).T


def solution(mesh):
    fine = Mesh(mesh.devices.reshape(X, ZL, CORE, Y, ZH), ("x", "zl", "core", "y", "zh"))
    seq, groups, every = ("x", "zl", "core"), ("x", "zl", "core", "zh"), ("x", "zl", "core", "y", "zh")
    return jax.shard_map(
        on_device,
        mesh=fine,
        in_specs=(
            P(every, None),
            P(None, every, None),
            P(),
            P(),
            P(None, "y", None, groups),
            P(None, "y", None, groups),
            P("y", None, groups),
            P(groups),
            P(groups, None),
            P(groups),
            P("y"),
            P("y"),
        ),
        out_specs=P(groups, "y"),
        check_vma=False,
    )
```

```python
import functools

import jax
import jax.numpy as jnp
from jax import lax
from jax.experimental import pallas as pl
from jax.experimental.pallas import tpu as pltpu
from jax.sharding import Mesh
from jax.sharding import PartitionSpec as P

D = 8192
HD = 128
MODES = 16
S = 512
LOG2E = 1.4426950408889634
SCALE2 = HD**-0.5 * LOG2E
X, ZL, CORE, Y, ZH = 4, 4, 2, 4, 2
Z = ZL * ZH
GROUPS = X * ZL * CORE * ZH
VPD = 2
ROWS = VPD * S
VOCAB = 512
TILE = 256
SPAN = 512
CHUNK = 128
STATS = 32
VMEM_LIMIT = 56 * 1024 * 1024


def params(**kw):
    return pltpu.CompilerParams(vmem_limit_bytes=VMEM_LIMIT, **kw)


def dot_t(a, b):
    return lax.dot_general(a, b, (((1,), (1,)), ((), ())), preferred_element_type=jnp.float32)


def state_kernel(lag_ref, x_ref, rate_ref, out_ref, x32):
    x32[...] = x_ref[...].astype(jnp.float32)
    rate = rate_ref[...]
    decay = jnp.exp(-rate)
    state = jnp.zeros_like(decay)
    for row in range(x_ref.shape[0]):
        state = state * decay + x32[row : row + 1, :]
    state = state * jnp.exp(-rate * lag_ref[0].astype(jnp.float32))
    for zl in range(2):
        for core in range(CORE):
            for zh in range(ZH):
                g = (zl * CORE + core) * ZH + zh
                out_ref[core, 0, zl, zh] = state[:, g * 128 : (g + 1) * 128]


def local_states(lag, prefix_input, rates_t):
    rows = prefix_input.shape[0]
    return pl.pallas_call(
        state_kernel,
        grid=(8,),
        in_specs=[
            pl.BlockSpec(memory_space=pltpu.SMEM),
            pl.BlockSpec((rows, 1024), lambda i: (0, i)),
            pl.BlockSpec((MODES, 1024), lambda i: (0, i)),
        ],
        out_specs=pl.BlockSpec((CORE, 1, 2, ZH, MODES, 128), lambda i: (0, i // 2, i % 2, 0, 0, 0)),
        out_shape=jax.ShapeDtypeStruct((CORE, X, ZL, ZH, MODES, 128), jnp.float32),
        scratch_shapes=[pltpu.VMEM((rows, 1024), jnp.float32)],
        compiler_params=params(),
        cost_estimate=pl.CostEstimate(flops=16 * 2**20, bytes_accessed=2 * 2**20, transcendentals=2**18),
        name="prefix_state",
    )(lag, prefix_input, rates_t)


def diagonal():
    return lax.broadcasted_iota(jnp.int32, (128, 128), 0) == lax.broadcasted_iota(jnp.int32, (128, 128), 1)


def split_terms(left):
    terms = []
    for _ in range(3):
        term = left.astype(jnp.bfloat16).astype(jnp.float32)
        terms.append(term)
        left = left - term
    return terms


def stats_block(lse):
    same = diagonal()
    lines = [
        jnp.sum(jnp.where(same, lse[i * 128 : (i + 1) * 128], 0.0), axis=0, keepdims=True)
        for i in range(ROWS // 128)
    ]
    terms = split_terms(jnp.concatenate(lines, axis=0))
    return jnp.concatenate(terms + [jnp.zeros_like(terms[0])], axis=0).astype(jnp.bfloat16)


def attend_kernel(*refs):
    count = (len(refs) - 1) // 2
    queries, kv_ref, outs = refs[:count], refs[count], refs[count + 1 :]
    per_span = SPAN // kv_ref.shape[2]
    running = [None] * count
    for j in range(kv_ref.shape[0] // per_span):
        shards = slice(j * per_span, (j + 1) * per_span)
        keys = kv_ref[shards, 0].reshape(SPAN, HD)
        values = kv_ref[shards, 1].reshape(SPAN, HD)
        for i in range(count):
            scores = dot_t(queries[i][...], keys)
            top = jnp.max(scores, axis=1, keepdims=True) * SCALE2
            if j > 0:
                best, denom, acc = running[i]
                top = jnp.maximum(best, top)
            weights = jnp.exp2(scores * SCALE2 - top)
            part = jnp.sum(weights, axis=1, keepdims=True)
            value = jnp.dot(weights.astype(jnp.bfloat16), values, preferred_element_type=jnp.float32)
            if j > 0:
                factor = jnp.exp2(best - top)
                part, value = denom * factor + part, acc * factor + value
            running[i] = (top, part, value)
    for out_ref, (best, denom, acc) in zip(outs, running):
        out_ref[:ROWS] = (acc / denom).astype(jnp.bfloat16)
        out_ref[ROWS:] = stats_block(best + jnp.log2(denom))


def attend(queries, kv):
    keys = kv.shape[0] * kv.shape[2]
    count = len(queries)
    return pl.pallas_call(
        attend_kernel,
        out_shape=[jax.ShapeDtypeStruct((ROWS + STATS, HD), jnp.bfloat16)] * count,
        compiler_params=params(),
        cost_estimate=pl.CostEstimate(
            flops=8 * count * ROWS * keys * HD,
            bytes_accessed=3 * 2**20,
            transcendentals=count * ROWS * keys,
        ),
        name="attend",
    )(*queries, kv)


def own_kernel(attn_ref, o_ref):
    lses = []
    for v in range(VPD):
        for i in range(S // TILE):
            rows = slice(i * TILE, (i + 1) * TILE)
            seen = (i + 1) * TILE
            scores = dot_t(attn_ref[0, v, rows], attn_ref[1, v, :seen]) * SCALE2
            q_pos = lax.broadcasted_iota(jnp.int32, (TILE, seen), 0) + i * TILE
            k_pos = lax.broadcasted_iota(jnp.int32, (TILE, seen), 1)
            scores = jnp.where(q_pos >= k_pos, scores, -jnp.inf)
            top = jnp.max(scores, axis=1, keepdims=True)
            weights = jnp.exp2(scores - top)
            denom = jnp.sum(weights, axis=1, keepdims=True)
            acc = jnp.dot(
                weights.astype(jnp.bfloat16), attn_ref[2, v, :seen], preferred_element_type=jnp.float32
            )
            out = slice(v * S + i * TILE, v * S + (i + 1) * TILE)
            o_ref[out] = (acc / denom).astype(jnp.bfloat16)
            lses.append(top + jnp.log2(denom))
    o_ref[ROWS:] = stats_block(jnp.concatenate(lses, axis=0))


def own_attention(suffix_attn):
    return pl.pallas_call(
        own_kernel,
        out_shape=jax.ShapeDtypeStruct((ROWS + STATS, HD), jnp.bfloat16),
        compiler_params=params(),
        cost_estimate=pl.CostEstimate(flops=2**28, bytes_accessed=2 * 2**20, transcendentals=2**19),
        name="own_attention",
    )(suffix_attn)


def conv_kernel(hyena_ref, resid_ref, rate_ref, amp_ref, base_ref, x32, y32):
    chunks = S // CHUNK
    lanes = VPD * chunks
    for v in range(VPD):
        x32[v * S : (v + 1) * S] = hyena_ref[1, v].astype(jnp.float32)
    decay, far = [], []
    for m in range(MODES):
        rate = jnp.broadcast_to(rate_ref[m : m + 1, :], (lanes, 128))
        decay.append(jnp.exp(-rate))
        far.append(jnp.exp(-rate * CHUNK))

    def first_pass(i, states):
        x = x32[pl.ds(i, lanes, stride=CHUNK), :]
        return tuple(s * d + x for s, d in zip(states, decay))

    zero = jnp.zeros((lanes, 128), jnp.float32)
    ends = lax.fori_loop(0, CHUNK, first_pass, (zero,) * MODES, unroll=8)
    chunk = lax.broadcasted_iota(jnp.int32, (lanes, 128), 0) % chunks
    starts = []
    for m in range(MODES):
        carried = zero
        for step in range(1, chunks):
            moved = pltpu.roll(carried * far[m] + ends[m], 1, axis=0)
            carried = jnp.where(chunk == step, moved, carried)
        starts.append(carried)

    amps = [jnp.broadcast_to(amp_ref[m : m + 1, :], (lanes, 128)) for m in range(MODES)]

    def second_pass(i, states):
        x = x32[pl.ds(i, lanes, stride=CHUNK), :]
        states = tuple(s * d + x for s, d in zip(states, decay))
        terms = [s * a for s, a in zip(states, amps)]
        while len(terms) > 1:
            terms = [a + b for a, b in zip(terms[::2], terms[1::2])]
        y32[pl.ds(i, lanes, stride=CHUNK), :] = terms[0]
        return states

    lax.fori_loop(0, CHUNK, second_pass, tuple(starts), unroll=8)
    for v in range(VPD):
        rows = slice(v * S, (v + 1) * S)
        base_ref[rows] = resid_ref[v].astype(jnp.float32) + hyena_ref[0, v].astype(jnp.float32) * y32[rows]


def conv_base(suffix_hyena, suffix_resid, rates, amps):
    return pl.pallas_call(
        conv_kernel,
        out_shape=jax.ShapeDtypeStruct((ROWS, HD), jnp.float32),
        scratch_shapes=[pltpu.VMEM((ROWS, HD), jnp.float32), pltpu.VMEM((ROWS, HD), jnp.float32)],
        compiler_params=params(),
        cost_estimate=pl.CostEstimate(flops=2**25, bytes_accessed=2 * 2**20, transcendentals=2**15),
        name="suffix_conv",
    )(suffix_hyena, suffix_resid, rates, amps)


def combine_kernel(base_ref, gain_ref, hyena_ref, rate_ref, amp_ref, state_ref, *refs):
    parts, out_ref, hid, squares, tail = refs[:-4], *refs[-4:]
    state = functools.reduce(jnp.add, [state_ref[k] for k in range(Z)])
    ahead = lax.broadcasted_iota(jnp.int32, (8, 128), 0).astype(jnp.float32) + 1.0
    terms, decay = [], []
    for m in range(MODES):
        rate = jnp.broadcast_to(rate_ref[m : m + 1, :], (8, 128))
        scale = amp_ref[m : m + 1, :] * state[m : m + 1, :]
        terms.append(scale * jnp.exp(-rate * ahead))
        decay.append(jnp.exp(-rate * 8.0))
    for k in range(S // 8):
        sums = terms
        while len(sums) > 1:
            sums = [p + q for p, q in zip(sums[::2], sums[1::2])]
        tail[k * 8 : k * 8 + 8] = sums[0]
        terms = [t * d for t, d in zip(terms, decay)]

    lses = []
    for ref in parts:
        stats = ref[ROWS:].astype(jnp.float32)
        lses.append(stats[:8] + stats[8:16] + stats[16:24])
    top = functools.reduce(jnp.maximum, lses)
    shares = [jnp.exp2(lse - top) for lse in lses]
    whole = functools.reduce(jnp.add, shares)
    factors = [(share / whole).T for share in shares]
    gain = gain_ref[...]
    for i in range(ROWS // 128):
        rows = slice(i * 128, (i + 1) * 128)
        v, at = i * 128 // S, i * 128 % S
        gate = hyena_ref[0, v, at : at + 128].astype(jnp.float32)
        hidden = base_ref[rows] + gate * tail[at : at + 128]
        for factor, ref in zip(factors, parts):
            hidden = hidden + factor[:, i : i + 1] * ref[rows].astype(jnp.float32)
        hid[rows] = hidden * gain
        squares[rows] = jnp.broadcast_to(jnp.sum(hidden * hidden, axis=1, keepdims=True), (128, 128))
    same = diagonal()
    for x in range(X):
        for core in range(CORE):
            columns = []
            for k in range(Z):
                g = ((x * ZL + k // ZH) * CORE + core) * ZH + k % ZH
                spots = [slice(v * S + g * 8, v * S + g * 8 + 8) for v in range(VPD)]
                pair = jnp.concatenate([hid[spot] for spot in spots], axis=0)
                out_ref[x * CORE + core, k * 16 : k * 16 + 16] = pair.astype(jnp.bfloat16)
                columns += [squares[spot] for spot in spots]
            line = jnp.sum(jnp.where(same, jnp.concatenate(columns, axis=0), 0.0), axis=0, keepdims=True)
            spare = jnp.zeros((13, 128), jnp.float32)
            rows = jnp.concatenate(split_terms(line) + [spare], axis=0)
            out_ref[x * CORE + core, 128:] = rows.astype(jnp.bfloat16)


def combine(base, gain, suffix_hyena, rates, amps, states, parts):
    whole = lambda a: pl.BlockSpec(a.shape, lambda i: (0,) * a.ndim)
    args = (base, gain, suffix_hyena, rates, amps, states, *parts)
    specs = [whole(a) for a in args]
    specs[2] = pl.BlockSpec((1, VPD, S, HD), lambda i: (0, 0, 0, 0))
    return pl.pallas_call(
        combine_kernel,
        grid=(1,),
        in_specs=specs,
        out_specs=pl.BlockSpec((X * CORE, 144, 128), lambda i: (0, 0, 0)),
        out_shape=jax.ShapeDtypeStruct((X * CORE, 144, 128), jnp.bfloat16),
        scratch_shapes=[pltpu.VMEM((rows, HD), jnp.float32) for rows in (ROWS, ROWS, S)],
        compiler_params=params(),
        cost_estimate=pl.CostEstimate(flops=2**22, bytes_accessed=3 * 2**20, transcendentals=2**14),
        name="combine",
    )(*args)


def logits_kernel(source_ref, hid_ref, *refs):
    reads, out_ref = refs[:-1], refs[-1]
    logits = jnp.zeros((128, VOCAB), jnp.float32)
    line = jnp.zeros((1, 128), jnp.float32)
    for k, ref in enumerate(reads):
        for c in range(CORE):
            block = hid_ref[source_ref[k * CORE + c]]
            logits = logits + jnp.dot(block[:128], ref[c], preferred_element_type=jnp.float32)
            line = line + jnp.sum(block[128:].astype(jnp.float32), axis=0, keepdims=True)
    sums = jnp.sum(jnp.where(diagonal(), line, 0.0), axis=1, keepdims=True)
    sums = jnp.broadcast_to(sums, (128, 128))
    high = sums.astype(jnp.bfloat16)
    low = (sums - high.astype(jnp.float32)).astype(jnp.bfloat16)
    for k in range(Z):
        rows = slice(k * 16, (k + 1) * 16)
        out_ref[k, :, :VOCAB] = logits[rows].astype(jnp.bfloat16)
        out_ref[k, :, VOCAB : VOCAB + 128] = high[rows]
        out_ref[k, :, VOCAB + 128 :] = low[rows]


def partial_logits(sources, hidden, reads):
    vmem = pl.BlockSpec(memory_space=pltpu.VMEM)
    return pl.pallas_call(
        logits_kernel,
        in_specs=[pl.BlockSpec(memory_space=pltpu.SMEM)] + [vmem] * (1 + len(reads)),
        out_shape=jax.ShapeDtypeStruct((Z, 16, VOCAB + 256), jnp.bfloat16),
        compiler_params=params(),
        cost_estimate=pl.CostEstimate(flops=2**27, bytes_accessed=2 * 2**20, transcendentals=0),
        name="partial_logits",
    )(sources, hidden, *reads)


def final_kernel(group_ref, next_ref, pos_ref, mut_ref, share_ref, out_ref):
    whole = jnp.zeros((16, VOCAB + 256), jnp.float32)
    for k in range(Z):
        whole = whole + share_ref[k].astype(jnp.float32)
    square_sum = whole[:, VOCAB : VOCAB + 1] + whole[:, VOCAB + 128 : VOCAB + 129]
    logits = whole[:, :VOCAB] * lax.rsqrt(square_sum * (1.0 / D) + 1e-5)
    top = jnp.max(logits, axis=1, keepdims=True)
    log_sum = top + jnp.log(jnp.sum(jnp.exp(logits - top), axis=1, keepdims=True))
    row = lax.broadcasted_iota(jnp.int32, (8, VOCAB), 0)
    token = lax.broadcasted_iota(jnp.int32, (8, VOCAB), 1)
    following = jnp.zeros((8, VOCAB), jnp.int32)
    for r in range(8):
        following = jnp.where(row == r, next_ref[r], following)
    position = row + group_ref[0] * 8
    here = lax.broadcasted_iota(jnp.int32, (8, 128), 0) == lax.broadcasted_iota(jnp.int32, (8, 128), 1)
    for v in range(VPD):
        target = jnp.where(position == pos_ref[v], mut_ref[v], following)
        rows = slice(v * 8, v * 8 + 8)
        picked = jnp.sum(jnp.where(token == target, logits[rows], 0.0), axis=1, keepdims=True)
        line = jnp.sum(jnp.where(here, picked - log_sum[rows], 0.0), axis=0, keepdims=True)
        out_ref[v : v + 1, :] = line[:, :8]


def finish(group, ref_next, mutation_pos, mutation_base, shares):
    smem = pl.BlockSpec(memory_space=pltpu.SMEM)
    return pl.pallas_call(
        final_kernel,
        in_specs=[smem] * 4 + [pl.BlockSpec(memory_space=pltpu.VMEM)],
        out_shape=jax.ShapeDtypeStruct((VPD, 8), jnp.float32),
        compiler_params=params(),
        name="finish",
    )(group, ref_next, mutation_pos, mutation_base, shares)


def ring(size, shift):
    return [(i, (i + shift) % size) for i in range(size)]


def paired(size, bit):
    return [(i, i ^ bit) for i in range(size)]


def pick(array, index, axis=0):
    return lax.dynamic_index_in_dim(array, index, axis, keepdims=False)


def halve(states, bit, partner, axis_name, axis, meanwhile=None):
    got = lax.ppermute(pick(states, 1 - bit, axis), axis_name, partner)
    if meanwhile is None:
        return pick(states, bit, axis) + got
    got, other = lax.optimization_barrier((got, meanwhile(states)))
    return pick(states, bit, axis) + got, other


def after(value, first):
    return lax.optimization_barrier((value, first))[0]


def on_device(
    prefix_input,
    prefix_cache,
    decay_rates,
    residues,
    suffix_hyena,
    suffix_attn,
    suffix_resid,
    norm_gain,
    readout,
    ref_next,
    mutation_pos,
    mutation_base,
):
    x, zl, core = lax.axis_index("x"), lax.axis_index("zl"), lax.axis_index("core")
    y, zh = lax.axis_index("y"), lax.axis_index("zh")
    group = ((x * ZL + zl) * CORE + core) * ZH + zh
    shard_rows = prefix_input.shape[0]
    key_shards = prefix_cache.reshape(2, shard_rows, GROUPS, HD).transpose(2, 0, 1, 3)
    kv = lax.all_to_all(key_shards, ("x", "zl", "core", "zh"), split_axis=0, concat_axis=0, tiled=True)

    queries = suffix_attn[0].reshape(ROWS, HD)
    others = [lax.ppermute(queries, "y", ring(Y, k)) for k in range(1, Y)]

    rates_t = decay_rates.T
    amps_t = residues.T
    first = (((x * ZL + zl) * CORE + core) * Y + y) * ZH + zh
    lag = shard_rows * (GROUPS * Y - 1 - first)
    states = local_states(lag.astype(jnp.int32).reshape(1), prefix_input, rates_t)
    own_rates = lax.dynamic_slice_in_dim(rates_t, group * 128, 128, 1)
    own_amps = lax.dynamic_slice_in_dim(amps_t, group * 128, 128, 1)
    state = halve(states, core, paired(CORE, 1), "core", 0)
    state = state.reshape(2, 2, Z, MODES, 128)
    state, own = halve(
        state, x % 2, paired(X, 1), "x", 1, lambda s: own_attention(after(suffix_attn, s))
    )
    state, base = halve(
        state,
        x // 2,
        paired(X, 2),
        "x",
        0,
        lambda s: conv_base(after(suffix_hyena, (s, others)), suffix_resid, own_rates, own_amps),
    )
    for bit in (1, 2):
        state = state + lax.ppermute(state, "y", paired(Y, bit))

    gain = norm_gain.reshape(1, HD)
    near = jnp.stack([readout, lax.ppermute(readout, "core", paired(CORE, 1))])
    reads = [near] + [lax.ppermute(near, "x", ring(X, k)) for k in range(1, X)]
    kv, reads, base, own, others, state = lax.optimization_barrier(
        (kv, reads, base, own, others, state)
    )

    parts = [own]
    for shifts in ((2,), (1, 3)):
        outs = attend([others[k - 1] for k in shifts], kv)
        if shifts == (2,):
            state = after(state, outs[0])
        for k, out in zip(shifts, outs):
            parts.append(lax.ppermute(out, "y", ring(Y, Y - k)))
    states = lax.all_to_all(state, ("zl", "zh"), split_axis=0, concat_axis=0, tiled=True)
    parts += attend([queries], kv)
    hidden = combine(base, gain, suffix_hyena, own_rates, own_amps, states, parts)
    hidden = lax.all_to_all(hidden, ("x", "core"), split_axis=0, concat_axis=0, tiled=True)
    sources = [(x + X - k) % X * CORE + (core if c == 0 else 1 - core) for k in range(X) for c in range(CORE)]
    shares = partial_logits(jnp.stack(sources).astype(jnp.int32), hidden, reads)
    shares = lax.all_to_all(shares, ("zl", "zh"), split_axis=0, concat_axis=0, tiled=True)
    group_id = group.astype(jnp.int32).reshape(1)
    return finish(group_id, ref_next, mutation_pos, mutation_base, shares).T


def solution(mesh):
    fine = Mesh(mesh.devices.reshape(X, ZL, CORE, Y, ZH), ("x", "zl", "core", "y", "zh"))
    seq, groups, every = ("x", "zl", "core"), ("x", "zl", "core", "zh"), ("x", "zl", "core", "y", "zh")
    return jax.shard_map(
        on_device,
        mesh=fine,
        in_specs=(
            P(every, None),
            P(None, every, None),
            P(),
            P(),
            P(None, "y", None, groups),
            P(None, "y", None, groups),
            P("y", None, groups),
            P(groups),
            P(groups, None),
            P(groups),
            P("y"),
            P("y"),
        ),
        out_specs=P(groups, "y"),
        check_vma=False,
    )
```

```python
import functools

import jax
import jax.numpy as jnp
from jax import lax
from jax.experimental import pallas as pl
from jax.experimental.pallas import tpu as pltpu
from jax.sharding import Mesh
from jax.sharding import PartitionSpec as P

D = 8192
HD = 128
MODES = 16
S = 512
LOG2E = 1.4426950408889634
SCALE2 = HD**-0.5 * LOG2E
X, ZL, CORE, Y, ZH = 4, 4, 2, 4, 2
Z = ZL * ZH
GROUPS = X * ZL * CORE * ZH
VPD = 2
ROWS = VPD * S
VOCAB = 512
TILE = 256
SPAN = 512
CHUNK = 128
STATS = 32
VMEM_LIMIT = 56 * 1024 * 1024
VMEM_SMALL = 24 * 1024 * 1024


def params(limit=VMEM_LIMIT):
    return pltpu.CompilerParams(vmem_limit_bytes=limit)


def dot_t(a, b):
    return lax.dot_general(a, b, (((1,), (1,)), ((), ())), preferred_element_type=jnp.float32)


def state_kernel(lag_ref, x_ref, rate_ref, out_ref, x32):
    x32[...] = x_ref[...].astype(jnp.float32)
    rate = rate_ref[...]
    decay = jnp.exp(-rate)
    state = jnp.zeros_like(decay)
    for row in range(x_ref.shape[0]):
        state = state * decay + x32[row : row + 1, :]
    state = state * jnp.exp(-rate * lag_ref[0].astype(jnp.float32))
    for zl in range(2):
        for core in range(CORE):
            for zh in range(ZH):
                g = (zl * CORE + core) * ZH + zh
                out_ref[core, 0, zl, zh] = state[:, g * 128 : (g + 1) * 128]


def local_states(lag, prefix_input, rates_t):
    rows = prefix_input.shape[0]
    return pl.pallas_call(
        state_kernel,
        grid=(8,),
        in_specs=[
            pl.BlockSpec(memory_space=pltpu.SMEM),
            pl.BlockSpec((rows, 1024), lambda i: (0, i)),
            pl.BlockSpec((MODES, 1024), lambda i: (0, i)),
        ],
        out_specs=pl.BlockSpec((CORE, 1, 2, ZH, MODES, 128), lambda i: (0, i // 2, i % 2, 0, 0, 0)),
        out_shape=jax.ShapeDtypeStruct((CORE, X, ZL, ZH, MODES, 128), jnp.float32),
        scratch_shapes=[pltpu.VMEM((rows, 1024), jnp.float32)],
        compiler_params=params(VMEM_SMALL),
        cost_estimate=pl.CostEstimate(flops=16 * 2**20, bytes_accessed=2 * 2**20, transcendentals=2**18),
        name="prefix_state",
    )(lag, prefix_input, rates_t)


def diagonal():
    return lax.broadcasted_iota(jnp.int32, (128, 128), 0) == lax.broadcasted_iota(jnp.int32, (128, 128), 1)


def split_terms(left):
    terms = []
    for _ in range(3):
        term = left.astype(jnp.bfloat16).astype(jnp.float32)
        terms.append(term)
        left = left - term
    return terms


def stats_block(lse):
    same = diagonal()
    lines = [
        jnp.sum(jnp.where(same, lse[i * 128 : (i + 1) * 128], 0.0), axis=0, keepdims=True)
        for i in range(ROWS // 128)
    ]
    terms = split_terms(jnp.concatenate(lines, axis=0))
    return jnp.concatenate(terms + [jnp.zeros_like(terms[0])], axis=0).astype(jnp.bfloat16)


def attend_kernel(*refs):
    count = (len(refs) - 1) // 2
    queries, kv_ref, outs = refs[:count], refs[count], refs[count + 1 :]
    per_span = SPAN // kv_ref.shape[2]
    running = [None] * count
    for j in range(kv_ref.shape[0] // per_span):
        shards = slice(j * per_span, (j + 1) * per_span)
        keys = kv_ref[shards, 0].reshape(SPAN, HD)
        values = kv_ref[shards, 1].reshape(SPAN, HD)
        for i in range(count):
            scores = dot_t(queries[i][...], keys)
            top = jnp.max(scores, axis=1, keepdims=True) * SCALE2
            if j > 0:
                best, denom, acc = running[i]
                top = jnp.maximum(best, top)
            weights = jnp.exp2(scores * SCALE2 - top)
            part = jnp.sum(weights, axis=1, keepdims=True)
            value = jnp.dot(weights.astype(jnp.bfloat16), values, preferred_element_type=jnp.float32)
            if j > 0:
                factor = jnp.exp2(best - top)
                part, value = denom * factor + part, acc * factor + value
            running[i] = (top, part, value)
    for out_ref, (best, denom, acc) in zip(outs, running):
        out_ref[:ROWS] = (acc / denom).astype(jnp.bfloat16)
        out_ref[ROWS:] = stats_block(best + jnp.log2(denom))


def attend(queries, kv):
    keys = kv.shape[0] * kv.shape[2]
    count = len(queries)
    return pl.pallas_call(
        attend_kernel,
        out_shape=[jax.ShapeDtypeStruct((ROWS + STATS, HD), jnp.bfloat16)] * count,
        compiler_params=params(),
        cost_estimate=pl.CostEstimate(
            flops=8 * count * ROWS * keys * HD,
            bytes_accessed=3 * 2**20,
            transcendentals=count * ROWS * keys,
        ),
        name="attend",
    )(*queries, kv)


def own_kernel(attn_ref, o_ref):
    lses = []
    for v in range(VPD):
        for i in range(S // TILE):
            rows = slice(i * TILE, (i + 1) * TILE)
            seen = (i + 1) * TILE
            scores = dot_t(attn_ref[0, v, rows], attn_ref[1, v, :seen]) * SCALE2
            q_pos = lax.broadcasted_iota(jnp.int32, (TILE, seen), 0) + i * TILE
            k_pos = lax.broadcasted_iota(jnp.int32, (TILE, seen), 1)
            scores = jnp.where(q_pos >= k_pos, scores, -jnp.inf)
            top = jnp.max(scores, axis=1, keepdims=True)
            weights = jnp.exp2(scores - top)
            denom = jnp.sum(weights, axis=1, keepdims=True)
            acc = jnp.dot(
                weights.astype(jnp.bfloat16), attn_ref[2, v, :seen], preferred_element_type=jnp.float32
            )
            out = slice(v * S + i * TILE, v * S + (i + 1) * TILE)
            o_ref[out] = (acc / denom).astype(jnp.bfloat16)
            lses.append(top + jnp.log2(denom))
    o_ref[ROWS:] = stats_block(jnp.concatenate(lses, axis=0))


def own_attention(suffix_attn):
    return pl.pallas_call(
        own_kernel,
        out_shape=jax.ShapeDtypeStruct((ROWS + STATS, HD), jnp.bfloat16),
        compiler_params=params(VMEM_SMALL),
        cost_estimate=pl.CostEstimate(flops=2**28, bytes_accessed=2 * 2**20, transcendentals=2**19),
        name="own_attention",
    )(suffix_attn)


def conv_kernel(hyena_ref, resid_ref, rate_ref, amp_ref, base_ref, x32, y32):
    chunks = S // CHUNK
    lanes = VPD * chunks
    for v in range(VPD):
        x32[v * S : (v + 1) * S] = hyena_ref[1, v].astype(jnp.float32)
    decay, far = [], []
    for m in range(MODES):
        rate = jnp.broadcast_to(rate_ref[m : m + 1, :], (lanes, 128))
        decay.append(jnp.exp(-rate))
        far.append(jnp.exp(-rate * CHUNK))

    def first_pass(i, states):
        x = x32[pl.ds(i, lanes, stride=CHUNK), :]
        return tuple(s * d + x for s, d in zip(states, decay))

    zero = jnp.zeros((lanes, 128), jnp.float32)
    ends = lax.fori_loop(0, CHUNK, first_pass, (zero,) * MODES, unroll=8)
    chunk = lax.broadcasted_iota(jnp.int32, (lanes, 128), 0) % chunks
    starts = []
    for m in range(MODES):
        carried = zero
        for step in range(1, chunks):
            moved = pltpu.roll(carried * far[m] + ends[m], 1, axis=0)
            carried = jnp.where(chunk == step, moved, carried)
        starts.append(carried)

    amps = [jnp.broadcast_to(amp_ref[m : m + 1, :], (lanes, 128)) for m in range(MODES)]

    def second_pass(i, states):
        x = x32[pl.ds(i, lanes, stride=CHUNK), :]
        states = tuple(s * d + x for s, d in zip(states, decay))
        terms = [s * a for s, a in zip(states, amps)]
        while len(terms) > 1:
            terms = [a + b for a, b in zip(terms[::2], terms[1::2])]
        y32[pl.ds(i, lanes, stride=CHUNK), :] = terms[0]
        return states

    lax.fori_loop(0, CHUNK, second_pass, tuple(starts), unroll=8)
    for v in range(VPD):
        rows = slice(v * S, (v + 1) * S)
        base_ref[rows] = resid_ref[v].astype(jnp.float32) + hyena_ref[0, v].astype(jnp.float32) * y32[rows]


def conv_base(suffix_hyena, suffix_resid, rates, amps):
    return pl.pallas_call(
        conv_kernel,
        out_shape=jax.ShapeDtypeStruct((ROWS, HD), jnp.float32),
        scratch_shapes=[pltpu.VMEM((ROWS, HD), jnp.float32), pltpu.VMEM((ROWS, HD), jnp.float32)],
        compiler_params=params(VMEM_SMALL),
        cost_estimate=pl.CostEstimate(flops=2**25, bytes_accessed=2 * 2**20, transcendentals=2**15),
        name="suffix_conv",
    )(suffix_hyena, suffix_resid, rates, amps)


def combine_kernel(base_ref, gain_ref, hyena_ref, rate_ref, amp_ref, state_ref, *refs):
    parts, out_ref, hid, squares, tail = refs[:-4], *refs[-4:]
    state = functools.reduce(jnp.add, [state_ref[k] for k in range(Z)])
    ahead = lax.broadcasted_iota(jnp.int32, (8, 128), 0).astype(jnp.float32) + 1.0
    terms, decay = [], []
    for m in range(MODES):
        rate = jnp.broadcast_to(rate_ref[m : m + 1, :], (8, 128))
        scale = amp_ref[m : m + 1, :] * state[m : m + 1, :]
        terms.append(scale * jnp.exp(-rate * ahead))
        decay.append(jnp.exp(-rate * 8.0))
    for k in range(S // 8):
        sums = terms
        while len(sums) > 1:
            sums = [p + q for p, q in zip(sums[::2], sums[1::2])]
        tail[k * 8 : k * 8 + 8] = sums[0]
        terms = [t * d for t, d in zip(terms, decay)]

    lses = []
    for ref in parts:
        stats = ref[ROWS:].astype(jnp.float32)
        lses.append(stats[:8] + stats[8:16] + stats[16:24])
    top = functools.reduce(jnp.maximum, lses)
    shares = [jnp.exp2(lse - top) for lse in lses]
    whole = functools.reduce(jnp.add, shares)
    factors = [(share / whole).T for share in shares]
    gain = gain_ref[...]
    for i in range(ROWS // 128):
        rows = slice(i * 128, (i + 1) * 128)
        v, at = i * 128 // S, i * 128 % S
        gate = hyena_ref[0, v, at : at + 128].astype(jnp.float32)
        hidden = base_ref[rows] + gate * tail[at : at + 128]
        for factor, ref in zip(factors, parts):
            hidden = hidden + factor[:, i : i + 1] * ref[rows].astype(jnp.float32)
        hid[rows] = hidden * gain
        squares[rows] = jnp.broadcast_to(jnp.sum(hidden * hidden, axis=1, keepdims=True), (128, 128))
    same = diagonal()
    for x in range(X):
        for core in range(CORE):
            columns = []
            for k in range(Z):
                g = ((x * ZL + k // ZH) * CORE + core) * ZH + k % ZH
                spots = [slice(v * S + g * 8, v * S + g * 8 + 8) for v in range(VPD)]
                pair = jnp.concatenate([hid[spot] for spot in spots], axis=0)
                out_ref[x * CORE + core, k * 16 : k * 16 + 16] = pair.astype(jnp.bfloat16)
                columns += [squares[spot] for spot in spots]
            line = jnp.sum(jnp.where(same, jnp.concatenate(columns, axis=0), 0.0), axis=0, keepdims=True)
            spare = jnp.zeros((13, 128), jnp.float32)
            rows = jnp.concatenate(split_terms(line) + [spare], axis=0)
            out_ref[x * CORE + core, 128:] = rows.astype(jnp.bfloat16)


def combine(base, gain, suffix_hyena, rates, amps, states, parts):
    whole = lambda a: pl.BlockSpec(a.shape, lambda i: (0,) * a.ndim)
    args = (base, gain, suffix_hyena, rates, amps, states, *parts)
    specs = [whole(a) for a in args]
    specs[2] = pl.BlockSpec((1, VPD, S, HD), lambda i: (0, 0, 0, 0))
    return pl.pallas_call(
        combine_kernel,
        grid=(1,),
        in_specs=specs,
        out_specs=pl.BlockSpec((X * CORE, 144, 128), lambda i: (0, 0, 0)),
        out_shape=jax.ShapeDtypeStruct((X * CORE, 144, 128), jnp.bfloat16),
        scratch_shapes=[pltpu.VMEM((rows, HD), jnp.float32) for rows in (ROWS, ROWS, S)],
        compiler_params=params(),
        cost_estimate=pl.CostEstimate(flops=2**22, bytes_accessed=3 * 2**20, transcendentals=2**14),
        name="combine",
    )(*args)


def logits_kernel(source_ref, hid_ref, *refs):
    reads, out_ref = refs[:-1], refs[-1]
    logits = jnp.zeros((128, VOCAB), jnp.float32)
    line = jnp.zeros((1, 128), jnp.float32)
    for k, ref in enumerate(reads):
        for c in range(CORE):
            block = hid_ref[source_ref[k * CORE + c]]
            logits = logits + jnp.dot(block[:128], ref[c], preferred_element_type=jnp.float32)
            line = line + jnp.sum(block[128:].astype(jnp.float32), axis=0, keepdims=True)
    sums = jnp.sum(jnp.where(diagonal(), line, 0.0), axis=1, keepdims=True)
    sums = jnp.broadcast_to(sums, (128, 128))
    high = sums.astype(jnp.bfloat16)
    low = (sums - high.astype(jnp.float32)).astype(jnp.bfloat16)
    for k in range(Z):
        rows = slice(k * 16, (k + 1) * 16)
        out_ref[k, :, :VOCAB] = logits[rows].astype(jnp.bfloat16)
        out_ref[k, :, VOCAB : VOCAB + 128] = high[rows]
        out_ref[k, :, VOCAB + 128 :] = low[rows]


def partial_logits(sources, hidden, reads):
    vmem = pl.BlockSpec(memory_space=pltpu.VMEM)
    return pl.pallas_call(
        logits_kernel,
        in_specs=[pl.BlockSpec(memory_space=pltpu.SMEM)] + [vmem] * (1 + len(reads)),
        out_shape=jax.ShapeDtypeStruct((Z, 16, VOCAB + 256), jnp.bfloat16),
        compiler_params=params(),
        cost_estimate=pl.CostEstimate(flops=2**27, bytes_accessed=2 * 2**20, transcendentals=0),
        name="partial_logits",
    )(sources, hidden, *reads)


def final_kernel(group_ref, next_ref, pos_ref, mut_ref, share_ref, out_ref):
    whole = jnp.zeros((16, VOCAB + 256), jnp.float32)
    for k in range(Z):
        whole = whole + share_ref[k].astype(jnp.float32)
    square_sum = whole[:, VOCAB : VOCAB + 1] + whole[:, VOCAB + 128 : VOCAB + 129]
    logits = whole[:, :VOCAB] * lax.rsqrt(square_sum * (1.0 / D) + 1e-5)
    top = jnp.max(logits, axis=1, keepdims=True)
    log_sum = top + jnp.log(jnp.sum(jnp.exp(logits - top), axis=1, keepdims=True))
    row = lax.broadcasted_iota(jnp.int32, (8, VOCAB), 0)
    token = lax.broadcasted_iota(jnp.int32, (8, VOCAB), 1)
    following = jnp.zeros((8, VOCAB), jnp.int32)
    for r in range(8):
        following = jnp.where(row == r, next_ref[r], following)
    position = row + group_ref[0] * 8
    here = lax.broadcasted_iota(jnp.int32, (8, 128), 0) == lax.broadcasted_iota(jnp.int32, (8, 128), 1)
    for v in range(VPD):
        target = jnp.where(position == pos_ref[v], mut_ref[v], following)
        rows = slice(v * 8, v * 8 + 8)
        picked = jnp.sum(jnp.where(token == target, logits[rows], 0.0), axis=1, keepdims=True)
        line = jnp.sum(jnp.where(here, picked - log_sum[rows], 0.0), axis=0, keepdims=True)
        out_ref[v : v + 1, :] = line[:, :8]


def finish(group, ref_next, mutation_pos, mutation_base, shares):
    smem = pl.BlockSpec(memory_space=pltpu.SMEM)
    return pl.pallas_call(
        final_kernel,
        in_specs=[smem] * 4 + [pl.BlockSpec(memory_space=pltpu.VMEM)],
        out_shape=jax.ShapeDtypeStruct((VPD, 8), jnp.float32),
        compiler_params=params(),
        name="finish",
    )(group, ref_next, mutation_pos, mutation_base, shares)


def ring(size, shift):
    return [(i, (i + shift) % size) for i in range(size)]


def paired(size, bit):
    return [(i, i ^ bit) for i in range(size)]


def pick(array, index, axis=0):
    return lax.dynamic_index_in_dim(array, index, axis, keepdims=False)


def halve(states, bit, partner, axis_name, axis, meanwhile=None):
    got = lax.ppermute(pick(states, 1 - bit, axis), axis_name, partner)
    if meanwhile is None:
        return pick(states, bit, axis) + got
    got, other = lax.optimization_barrier((got, meanwhile(states)))
    return pick(states, bit, axis) + got, other


def after(value, first):
    return lax.optimization_barrier((value, first))[0]


def on_device(
    prefix_input,
    prefix_cache,
    decay_rates,
    residues,
    suffix_hyena,
    suffix_attn,
    suffix_resid,
    norm_gain,
    readout,
    ref_next,
    mutation_pos,
    mutation_base,
):
    x, zl, core = lax.axis_index("x"), lax.axis_index("zl"), lax.axis_index("core")
    y, zh = lax.axis_index("y"), lax.axis_index("zh")
    group = ((x * ZL + zl) * CORE + core) * ZH + zh
    shard_rows = prefix_input.shape[0]
    key_shards = prefix_cache.reshape(2, shard_rows, GROUPS, HD).transpose(2, 0, 1, 3)
    kv = lax.all_to_all(key_shards, ("x", "zl", "core", "zh"), split_axis=0, concat_axis=0, tiled=True)

    queries = suffix_attn[0].reshape(ROWS, HD)
    others = [lax.ppermute(queries, "y", ring(Y, k)) for k in range(1, Y)]

    rates_t = decay_rates.T
    amps_t = residues.T
    first = (((x * ZL + zl) * CORE + core) * Y + y) * ZH + zh
    lag = shard_rows * (GROUPS * Y - 1 - first)
    states = local_states(lag.astype(jnp.int32).reshape(1), prefix_input, rates_t)
    own_rates = lax.dynamic_slice_in_dim(rates_t, group * 128, 128, 1)
    own_amps = lax.dynamic_slice_in_dim(amps_t, group * 128, 128, 1)
    state = halve(states, core, paired(CORE, 1), "core", 0)
    state = state.reshape(2, 2, Z, MODES, 128)
    state, own = halve(
        state, x % 2, paired(X, 1), "x", 1, lambda s: own_attention(after(suffix_attn, s))
    )
    state, base = halve(
        state,
        x // 2,
        paired(X, 2),
        "x",
        0,
        lambda s: conv_base(after(suffix_hyena, (s, others)), suffix_resid, own_rates, own_amps),
    )
    for bit in (1, 2):
        state = state + lax.ppermute(state, "y", paired(Y, bit))

    gain = norm_gain.reshape(1, HD)
    near = jnp.stack([readout, lax.ppermute(readout, "core", paired(CORE, 1))])
    reads = [near] + [lax.ppermute(near, "x", ring(X, k)) for k in range(1, X)]
    kv, reads, base, own, others, state = lax.optimization_barrier(
        (kv, reads, base, own, others, state)
    )

    parts = [own]
    for shifts in ((2,), (1, 3)):
        outs = attend([others[k - 1] for k in shifts], kv)
        if shifts == (2,):
            state = after(state, outs[0])
        for k, out in zip(shifts, outs):
            parts.append(lax.ppermute(out, "y", ring(Y, Y - k)))
    states = lax.all_to_all(state, ("zl", "zh"), split_axis=0, concat_axis=0, tiled=True)
    parts += attend([queries], kv)
    hidden = combine(base, gain, suffix_hyena, own_rates, own_amps, states, parts)
    hidden = lax.all_to_all(hidden, ("x", "core"), split_axis=0, concat_axis=0, tiled=True)
    sources = [(x + X - k) % X * CORE + (core if c == 0 else 1 - core) for k in range(X) for c in range(CORE)]
    shares = partial_logits(jnp.stack(sources).astype(jnp.int32), hidden, reads)
    shares = lax.all_to_all(shares, ("zl", "zh"), split_axis=0, concat_axis=0, tiled=True)
    group_id = group.astype(jnp.int32).reshape(1)
    return finish(group_id, ref_next, mutation_pos, mutation_base, shares).T


def solution(mesh):
    fine = Mesh(mesh.devices.reshape(X, ZL, CORE, Y, ZH), ("x", "zl", "core", "y", "zh"))
    seq, groups, every = ("x", "zl", "core"), ("x", "zl", "core", "zh"), ("x", "zl", "core", "y", "zh")
    return jax.shard_map(
        on_device,
        mesh=fine,
        in_specs=(
            P(every, None),
            P(None, every, None),
            P(),
            P(),
            P(None, "y", None, groups),
            P(None, "y", None, groups),
            P("y", None, groups),
            P(groups),
            P(groups, None),
            P(groups),
            P("y"),
            P("y"),
        ),
        out_specs=P(groups, "y"),
        check_vma=False,
    )
```
